32 devices in a mesh: group: 2 (over y), expert: 4 (over z), dp: 4 (over x, core).
Axes of the slice: x: 2, y: 2, z: 4, core: 2. Of those that a mesh axis runs over, the one named last changes fastest.
Arguments:
- tokens: bfloat16 [1024, 2048], P(('group', 'expert', 'dp')), parts along dimension 0, may hold values from -6 to 6
- out_grad: bfloat16 [1024, 2048], P(('group', 'expert', 'dp')), parts along dimension 0, may hold values from -0.59765625 to 0.59765625
- expert_ids: int32 [1024, 2], P(('group', 'expert', 'dp')), parts along dimension 0, may hold values from 0 to 3, all different within a row; in each aligned block of 32 rows (0 to 31, 32 to 63, ...) at most 24 rows name the same one
- combine: float32 [1024, 2], P(('group', 'expert', 'dp')), parts along dimension 0, may hold values from 0.1 to 0.6
- gate_weight: bfloat16 [4, 2048, 768], P('expert', 'dp'), may hold values from -0.125 to 0.125
- up_weight: bfloat16 [4, 2048, 768], P('expert', 'dp'), may hold values from -0.125 to 0.125
- down_t: bfloat16 [4, 2048, 768], P('expert', 'dp'), may hold values from -0.21875 to 0.21875
Outputs:
- mixed: bfloat16 [1024, 2048], P(('group', 'expert', 'dp')), parts along dimension 0
- down_grad: bfloat16 [8, 2048, 768], P(('group', 'expert'), 'dp'), parts along dimension 0
The draws below stay inside these ranges and needn't reach their ends.
There are 2 independent parts, one for each index of `group`. The reference program is written for one: setup_inputs(seed, part) draws one part's arguments, and reference() takes and returns one part's arrays. A program takes and returns all parts, laid end to end along the dimension named above; an argument that names none is the same for every part. Nothing has to cross between parts.
Inputs may be any that keep to these rules, and one draw needn't show every extreme that they name: `expert_ids`: each row names 2 different experts. Among the 32 tokens of one device no expert is named by more than 24 of them, and in every draw some expert is named by exactly 24 tokens of some device.
All inputs are finite; a program needn't handle non-finite values.
Results may differ from the reference program's by a relative error of at most 0.012.
Values may be sent and summed in bfloat16 or wider, within the bound.
A program may use at most 64 MiB of HBM per device.

```python
import math
import jax
import jax.numpy as jnp
import numpy as np
from jax import lax

D = 2048
FF = 768
TOK_DEV = 32
CAP = 24
EXPERTS = 4
TOP = 2
TOKENS = 512
N_EXPERT = 4
N_DP = 4


def spiked(drawn, stream_key, source, target, shards_of, factor):
    def block_of(dim):
        return (jnp.arange(drawn.shape[dim]) // (drawn.shape[dim] // shards_of)).reshape((-1,) + (1,) * (drawn.ndim - 1 - dim))

    first = jax.random.permutation(stream_key, shards_of)[block_of(target)]
    other_side = (block_of(target) + shards_of // 2) % shards_of
    return jnp.where((block_of(source) == first) | (block_of(source) == other_side), factor * drawn, drawn)


def block_levels(key, dims, split, low, top_value):
    gain, own = 1.0, jax.random.fold_in(key, 6)
    for axis_at, parts in split:
        draws = jnp.exp(jax.random.uniform(jax.random.fold_in(own, axis_at), (parts,), jnp.float32, low / len(split), top_value / len(split)))
        gain = gain * jnp.repeat(draws, dims[axis_at] // parts).reshape([-1 if axis == axis_at else 1 for axis in range(len(dims))])
    return gain


def assign_block(stream_key, own, number, rows, amount, top, bound, lean):
    order = jax.random.permutation(stream_key, amount)
    packed, usual = shares(amount, rows * top, bound, lean, True), shares(amount, rows * top, bound, lean, False)
    places = jnp.arange(amount)

    def named(tallies, rotation):
        used = int((tallies > 0).sum())
        fixed = max(1, used // 4)
        passed = fixed + (places - fixed + rotation * (used - fixed)) % max(1, amount - fixed)
        return jnp.zeros((amount,), jnp.int32).at[order[jnp.where(places < fixed, places, passed)]].set(jnp.asarray(tallies, jnp.int32))

    tallies = jnp.where(number % 4 == 0, named(packed, number // 4), named(usual, number - number // 4 - 1))
    mixed = jax.random.permutation(jax.random.fold_in(own, 3), amount)
    giver, sink = mixed[0:amount // 2 * 2:2], mixed[1:amount // 2 * 2:2]
    slack = jnp.minimum(tallies[giver] - 1, bound - tallies[sink]) // 2
    slack = jnp.where((giver == order[0]) | (sink == order[0]) | (tallies[sink] == 0), 0, jnp.maximum(slack, 0))
    passed = jax.random.randint(jax.random.fold_in(own, 4), (amount // 2,), 0, 1 << 20) % (slack + 1)
    tallies = tallies.at[giver].add(-passed).at[sink].add(passed)
    items = jnp.searchsorted(jnp.cumsum(tallies), jnp.arange(rows * top), side="right").astype(jnp.int32)
    table = items.reshape(top, rows).T
    table = table[jax.random.permutation(jax.random.fold_in(own, 1), rows)]
    rotation = jax.random.randint(jax.random.fold_in(own, 2), (rows, 1), 0, top)
    return jnp.take_along_axis(table, (jnp.arange(top)[None, :] + rotation) % top, axis=1)


def shares(count, total, reach, lean, full):
    portions = [(1 << 20) // math.isqrt(rank ** lean) + 1 for rank in range(1, count + 1)]
    largest = reach if full else min(reach, max(-(-total // count), total * portions[0] // sum(portions)))
    least = 1 if total - largest >= count - 1 else 0
    holding, rest = [largest] + [least] * (count - 1), total - largest - least * (count - 1)
    while rest > 0:
        free = [i for i in range(1, count) if holding[i] < largest] or [i for i in range(1, count) if holding[i] < reach]
        whole, budget = sum([portions[i] for i in free]), rest
        for i in free:
            extra = min(reach - holding[i], max(1, budget * portions[i] // whole), rest)
            holding[i] = holding[i] + extra
            rest = rest - extra
    return np.array(holding)


def noise(own_key, dims, width, limit, pieces=(), held_as=jnp.bfloat16):
    loudness = block_levels(own_key, dims, pieces, -0.22, 0.18) if pieces else 1.0
    entries = jax.random.normal(own_key, dims, jnp.float32) * width * loudness
    return jnp.minimum(jnp.maximum(entries, -limit), limit).astype(held_as)


def bell_draw_with(rng, extent, deviation, reach, cuts, heavy, kind=jnp.bfloat16):
    entries = deviation * jax.random.normal(rng, extent, jnp.float32)
    if cuts:
        entries = entries * block_levels(rng, extent, cuts, -0.22, 0.18)
    return jnp.clip(spiked(entries, jax.random.fold_in(rng, 3), *heavy), -reach, reach).astype(kind)


def setup_inputs(seed: int = 0, part: int = 0) -> dict:
    streams_of = jax.random.split(jax.random.key(seed), 8)
    part_keys = jax.random.split(jax.random.fold_in(streams_of[7], part), 8)
    tokens = noise(part_keys[0], (TOKENS, D), 1.0, 6.0, ((0, 16),))
    out_grad = bell_draw_with(part_keys[1], (TOKENS, D), 0.1, 0.59765625, ((0, 16),), (0, 1, 16, 2.0))
    expert_ids_keys = jax.random.split(jax.random.fold_in(part_keys[2], 1), TOKENS // TOK_DEV)
    expert_ids_turns = jax.random.permutation(jax.random.fold_in(part_keys[2], 3), TOKENS // TOK_DEV)
    expert_ids = jax.vmap(lambda own, number: assign_block(jax.random.fold_in(part_keys[2], 2), own, number, TOK_DEV, EXPERTS, TOP, CAP, 2))(expert_ids_keys, expert_ids_turns).reshape((TOKENS, TOP))
    combine = jnp.clip(0.1 + 0.5 * jax.random.uniform(part_keys[3], (TOKENS, TOP), jnp.float32) ** block_levels(part_keys[3], (TOKENS, TOP), ((0, 16),), -0.2, 0.2), 0.1, 0.6)
    gate_weight = noise(streams_of[4], (EXPERTS, D, FF), D ** -0.5, 0.125, ((0, 4), (1, 4)))
    up_weight = noise(streams_of[5], (EXPERTS, D, FF), D ** -0.5, 0.125, ((0, 4), (1, 4)))
    down_t = noise(streams_of[6], (EXPERTS, D, FF), FF ** -0.5, 0.21875, ((0, 4), (1, 4)))
    return {"tokens": tokens, "out_grad": out_grad, "expert_ids": expert_ids, "combine": combine, "gate_weight": gate_weight, "up_weight": up_weight, "down_t": down_t}


def reference(tokens, out_grad, expert_ids, combine, gate_weight, up_weight, down_t):
    blocks = TOKENS // TOK_DEV
    pairs = TOK_DEV * TOP
    route_ids = expert_ids.reshape(blocks, pairs)
    onehot = (route_ids[:, :, None] == jnp.arange(EXPERTS, dtype=jnp.int32)[None, None, :]).astype(jnp.int32)
    earlier = jnp.sum((jnp.cumsum(onehot, 1) - onehot) * onehot, 2)
    target = route_ids * CAP + earlier
    token_index = jnp.arange(TOKENS, dtype=jnp.int32).reshape(blocks, TOK_DEV)
    sources = jnp.repeat(token_index, TOP, axis=1)
    position = (jnp.arange(blocks, dtype=jnp.int32)[:, None] * (EXPERTS * CAP) + target).reshape(-1)
    slot_token = jnp.full((blocks * EXPERTS * CAP,), TOKENS, jnp.int32).at[position].set(sources.reshape(-1))
    slot_weight = jnp.zeros((blocks * EXPERTS * CAP,), jnp.float32).at[position].set(combine.reshape(-1))
    slot_token = slot_token.reshape(blocks, EXPERTS, CAP).transpose(1, 0, 2)
    slot_weight = slot_weight.reshape(blocks, EXPERTS, CAP).transpose(1, 0, 2)
    padded_rows = jnp.concatenate([tokens, jnp.zeros((1, D), jnp.bfloat16)], 0)
    padded_grad = jnp.concatenate([out_grad, jnp.zeros((1, D), jnp.bfloat16)], 0)

    def per_expert(running, inputs):
        token_slots, weight_slots, gate_w, up_w, down_w = inputs
        flat_slots = token_slots.reshape(-1)
        flat_weight = weight_slots.reshape(-1)
        expert_rows = padded_rows[flat_slots]
        gate_sum = jnp.dot(expert_rows, gate_w, preferred_element_type=jnp.float32)
        up_sum = jnp.dot(expert_rows, up_w, preferred_element_type=jnp.float32)
        hidden = (jax.nn.silu(gate_sum) * up_sum).astype(jnp.bfloat16)
        expert_out = jnp.dot(hidden, down_w.T, preferred_element_type=jnp.float32).astype(jnp.bfloat16)
        running = running.at[flat_slots].add(flat_weight[:, None] * expert_out.astype(jnp.float32))
        slot_grad = (flat_weight[:, None] * padded_grad[flat_slots].astype(jnp.float32)).astype(jnp.bfloat16)
        grad_rows = slot_grad.reshape(N_EXPERT, N_DP, CAP, D).transpose(1, 0, 2, 3).reshape(N_DP, N_EXPERT * CAP, D)
        hid_rows = hidden.reshape(N_EXPERT, N_DP, CAP, FF).transpose(1, 0, 2, 3).reshape(N_DP, N_EXPERT * CAP, FF)
        partial_value = jnp.einsum('jrd,jrf->jdf', grad_rows.astype(jnp.float32), hid_rows.astype(jnp.float32)).astype(jnp.bfloat16)
        down_grad = jnp.sum(partial_value.astype(jnp.float32), 0).astype(jnp.bfloat16)
        return running, down_grad

    start = jnp.zeros((TOKENS + 1, D), jnp.float32)
    running, down_grad = lax.scan(per_expert, start, (slot_token, slot_weight, gate_weight, up_weight, down_t))
    mixed = running[:TOKENS].astype(jnp.bfloat16)
    return mixed, down_grad
```

```python
import functools

import jax
import jax.numpy as jnp
from jax import lax
from jax.experimental import pallas as pl
from jax.experimental.pallas import tpu as pltpu
from jax.sharding import PartitionSpec as P

CAP = 24
MESH = pl.DeviceIdType.MESH
F32 = jnp.float32
BF16 = jnp.bfloat16


def dot(a, b, dims=((1,), (0,))):
    return lax.dot_general(a, b, (dims, ((), ())), preferred_element_type=F32)


def kernel(
    experts,
    replicas,
    tokens,
    out_grad,
    expert_ids,
    combine,
    gate_hbm,
    up_hbm,
    down_hbm,
    mixed,
    down_grad,
    gate_w,
    up_w,
    down_w,
    tok_send,
    tok_recv,
    grad_send,
    grad_recv,
    ret_send,
    ret_recv,
    mate_send,
    mate_recv,
    cross_send,
    cross_recv,
    own_sum,
    hid,
    load_sem,
    tok_ssem,
    tok_rsem,
    grad_ssem,
    grad_rsem,
    ret_ssem,
    ret_rsem,
    mate_ssem,
    mate_rsem,
    cross_ssem,
    cross_rsem,
    hid_ssem,
    hid_rsem,
    fwd_ssem,
    fwd_rsem,
):
    width = gate_hbm.shape[0]
    half = width // 2
    ff = gate_hbm.shape[1]
    rows = experts * CAP
    chips = replicas // 2
    e = lax.axis_index("expert")
    r = lax.axis_index("dp")
    chip = r // 2
    core = r % 2
    me = r * experts + e
    mate = {"dp": chip * 2 + 1 - core}

    loads = [
        pltpu.make_async_copy(src, dst, load_sem.at[i])
        for i, (src, dst) in enumerate(((gate_hbm, gate_w), (up_hbm, up_w), (down_hbm, down_w)))
    ]
    for load in loads:
        load.start()

    peers = []
    for dr in range(replicas):
        for de in range(experts):
            if dr or de:
                pe, pr = lax.rem(e + de, experts), lax.rem(r + dr, replicas)
                peers.append((pe, pr, pr * experts + pe))
    barrier = pltpu.get_barrier_semaphore()
    for pe, pr, _ in peers:
        pl.semaphore_signal(barrier, inc=1, device_id={"expert": pe, "dp": pr}, device_id_type=MESH)

    def exchange(src, dst, ssem, rsem):
        copies = []
        for pe, pr, n in peers:
            copies.append(
                (
                    pltpu.make_async_remote_copy(
                        src_ref=src.at[n],
                        dst_ref=dst.at[me],
                        send_sem=ssem.at[n],
                        recv_sem=rsem.at[me],
                        device_id={"expert": pe, "dp": pr},
                        device_id_type=MESH,
                    ),
                    pltpu.make_async_remote_copy(
                        src_ref=src.at[n],
                        dst_ref=dst.at[n],
                        send_sem=ssem.at[n],
                        recv_sem=rsem.at[n],
                        device_id={"expert": pe, "dp": pr},
                        device_id_type=MESH,
                    ),
                )
            )
        return copies

    def slab(block):
        return jnp.concatenate([block[:, :half], block[:, half:]], 0).astype(BF16)

    def fill(dst, value):
        for pr in range(replicas):
            for pe in range(experts):
                dst[pr * experts + pe] = slab(
                    value[pe * CAP : (pe + 1) * CAP, pr * width : (pr + 1) * width]
                )

    tok_count = tokens.shape[0]
    top = expert_ids.shape[1]
    column = lax.broadcasted_iota(jnp.int32, (tok_count, rows), 1)
    owner = jnp.zeros((tok_count, rows), jnp.int32)
    for j in range(1, experts):
        owner = owner + (column >= j * CAP).astype(jnp.int32)
    place = (column - owner * CAP).astype(F32)
    picks = [(expert_ids[:, k : k + 1] == owner).astype(F32) for k in range(top)]
    named = functools.reduce(jnp.add, picks)
    earlier = (
        lax.broadcasted_iota(jnp.int32, (tok_count, tok_count), 0)
        > lax.broadcasted_iota(jnp.int32, (tok_count, tok_count), 1)
    ).astype(F32)
    slot = dot(earlier.astype(BF16), named.astype(BF16))
    here = jnp.where(slot == place, 1.0, 0.0)
    choice = jnp.concatenate([pick * here for pick in picks], 0).astype(BF16)
    either = (named * here).astype(BF16)
    fill(tok_send, dot(either, tokens[...], ((0,), (0,))))
    pl.semaphore_wait(barrier, len(peers))

    tok_copies = exchange(tok_send, tok_recv, tok_ssem, tok_rsem)
    for out, _ in tok_copies:
        out.start()
    tok_recv[pl.ds(me, 1)] = tok_send[pl.ds(me, 1)]
    grad = out_grad[...].astype(F32)
    weighted = jnp.concatenate(
        [(combine[:, k : k + 1] * grad).astype(BF16) for k in range(top)], 0
    )
    fill(grad_send, dot(choice, weighted, ((0,), (0,))))
    grad_recv[pl.ds(me, 1)] = grad_send[pl.ds(me, 1)]
    for load in loads[:2]:
        load.wait()
    for out, back in tok_copies:
        back.wait_recv()
    grad_copies = exchange(grad_send, grad_recv, grad_ssem, grad_rsem)
    for out, _ in grad_copies:
        out.start()

    def mate_copy(c):
        return pltpu.make_async_remote_copy(
            src_ref=mate_send.at[c],
            dst_ref=mate_recv.at[c],
            send_sem=mate_ssem.at[c],
            recv_sem=mate_rsem.at[c],
            device_id=mate,
            device_id_type=MESH,
        )

    pair = 2 * experts
    other_chips = [lax.rem(chip + d, chips) for d in range(1, chips)]
    for d in list(range(1, chips)) + [0]:
        c = lax.rem(chip + d, chips)
        for j in range(2):
            at = pl.ds((c * 2 + j) * experts, experts)
            x = tok_recv[at]
            lo, hi = x[:, :CAP].reshape(rows, half), x[:, CAP:].reshape(rows, half)
            for i, w in enumerate((gate_w, up_w)):
                part = dot(lo, w[:half]) + dot(hi, w[half:])

                @pl.when(core == j)
                def _():
                    own_sum[d, i] = part

                @pl.when(core != j)
                def _():
                    mate_send[d, i] = part.astype(BF16)

        mate_copy(d).start()

    def cross_copy(d):
        return pltpu.make_async_remote_copy(
            src_ref=cross_send.at[d],
            dst_ref=cross_recv.at[d],
            send_sem=cross_ssem.at[d],
            recv_sem=cross_rsem.at[d],
            device_id={"dp": lax.rem(chip + d, chips) * 2 + core},
            device_id_type=MESH,
        )

    for d in range(1, chips):
        mate_copy(d).wait_recv()
        cross_send[d] = (own_sum[d] + mate_recv[d].astype(F32)).astype(BF16)
        cross_copy(d).start()
    mate_copy(0).wait_recv()
    total = own_sum[0] + mate_recv[0].astype(F32)
    own_sum[0] = total
    for d in range(1, chips):
        cross_copy(d).wait_recv()
    total = own_sum[0]
    for d in range(1, chips):
        total = total + cross_recv[d].astype(F32)
    gate, up = total[0], total[1]
    hid[pl.ds(r, 1)] = ((gate / (1.0 + jnp.exp(-gate))) * up).astype(BF16)[None]

    def hid_copy(d, src, at, target, ssem, rsem):
        return pltpu.make_async_remote_copy(
            src_ref=hid.at[src],
            dst_ref=hid.at[at],
            send_sem=ssem.at[d],
            recv_sem=rsem.at[d],
            device_id={"dp": target},
            device_id_type=MESH,
        )

    hid_out, hid_in = [], []
    for d in range(1, chips):
        ahead = lax.rem(chip + d, chips) * 2 + core
        behind = lax.rem(chip + chips - d, chips) * 2 + core
        hid_out.append(hid_copy(d, r, r, ahead, hid_ssem, hid_rsem))
        hid_in.append(hid_copy(d, r, behind, ahead, hid_ssem, hid_rsem))
    for copy in hid_out:
        copy.start()
    mate_r = chip * 2 + 1 - core
    mate_out = hid_copy(0, r, r, mate_r, fwd_ssem, fwd_rsem)
    mate_in = hid_copy(0, r, mate_r, mate_r, fwd_ssem, fwd_rsem)
    mate_out.start()
    loads[2].wait()

    ret_copies = exchange(ret_send, ret_recv, ret_ssem, ret_rsem)

    def give_back(pr):
        out = dot(hid[pr], down_w[...], ((1,), (1,)))
        for pe in range(experts):
            ret_send[pr * experts + pe] = slab(out[pe * CAP : (pe + 1) * CAP])

    def send_back(dr_pr, skip_self):
        for de in range(experts):
            if skip_self and de == 0:
                continue
            pe = lax.rem(e + de, experts)
            n = dr_pr * experts + pe
            pltpu.make_async_remote_copy(
                src_ref=ret_send.at[n],
                dst_ref=ret_recv.at[me],
                send_sem=ret_ssem.at[n],
                recv_sem=ret_rsem.at[me],
                device_id={"expert": pe, "dp": dr_pr},
                device_id_type=MESH,
            ).start()

    give_back(r)
    send_back(r, True)
    ret_recv[pl.ds(me, 1)] = ret_send[pl.ds(me, 1)]
    mate_in.wait_recv()
    give_back(mate_r)
    send_back(mate_r, False)
    forwards = []
    for d in range(1, chips):
        hid_in[d - 1].wait_recv()
        behind = lax.rem(chip + chips - d, chips)
        out = hid_copy(d, behind * 2 + core, behind * 2 + core, mate_r, fwd_ssem, fwd_rsem)
        into = hid_copy(d, behind * 2 + core, behind * 2 + 1 - core, mate_r, fwd_ssem, fwd_rsem)
        out.start()
        forwards.append((out, into))
        give_back(behind * 2 + core)
        send_back(behind * 2 + core, False)
    for d in range(1, chips):
        forwards[d - 1][1].wait_recv()
        behind = lax.rem(chip + chips - d, chips)
        give_back(behind * 2 + 1 - core)
        send_back(behind * 2 + 1 - core, False)

    for _, back in grad_copies:
        back.wait_recv()
    hidden = hid[...].reshape(replicas * rows, ff)
    for h in range(2):
        g = grad_recv[:, h * CAP : (h + 1) * CAP].reshape(replicas * rows, half)
        down_grad[h * half : (h + 1) * half] = dot(g, hidden, ((0,), (0,))).astype(BF16)

    for _, back in ret_copies:
        back.wait_recv()
    for pr in range(replicas):
        for h in range(2):
            block = ret_recv[pr * experts : (pr + 1) * experts, h * CAP : (h + 1) * CAP]
            got = dot(choice, block.reshape(rows, half))
            value = combine[:, 0:1] * got[:tok_count]
            for k in range(1, top):
                value = value + combine[:, k : k + 1] * got[k * tok_count : (k + 1) * tok_count]
            start = pr * width + h * half
            mixed[:, start : start + half] = value.astype(BF16)

    for copies in (tok_copies, grad_copies, ret_copies):
        for out, _ in copies:
            out.wait_send()
    for d in range(chips):
        mate_copy(d).wait_send()
    for d in range(1, chips):
        cross_copy(d).wait_send()
    for copy in hid_out:
        copy.wait_send()
    mate_out.wait_send()
    for out, _ in forwards:
        out.wait_send()


def tokens_move(tokens, out_grad, expert_ids, combine, gate_weight, up_weight, down_t):
    experts, replicas = lax.axis_size("expert"), lax.axis_size("dp")
    _, width, ff = gate_weight.shape
    peers, chips, rows = experts * replicas, replicas // 2, experts * CAP
    slabs = pltpu.VMEM((peers, 2 * CAP, width // 2), BF16)
    dma = pltpu.SemaphoreType.DMA
    vmem = pl.BlockSpec(memory_space=pltpu.VMEM)
    hbm = pl.BlockSpec(memory_space=pl.ANY)
    mixed, down_grad = pl.pallas_call(
        functools.partial(kernel, experts, replicas),
        out_shape=(
            jax.ShapeDtypeStruct(tokens.shape, BF16),
            jax.ShapeDtypeStruct((width, ff), BF16),
        ),
        in_specs=[vmem] * 4 + [hbm] * 3,
        out_specs=(vmem, vmem),
        scratch_shapes=[pltpu.VMEM((width, ff), BF16)] * 3
        + [slabs] * 6
        + [pltpu.VMEM((chips, 2, rows, ff), BF16)] * 4
        + [pltpu.VMEM((chips, 2, rows, ff), F32), pltpu.VMEM((replicas, rows, ff), BF16)]
        + [dma((3,))]
        + [dma((peers,))] * 6
        + [dma((chips,))] * 8,
        compiler_params=pltpu.CompilerParams(
            collective_id=0, has_side_effects=True, vmem_limit_bytes=40 * 1024 * 1024
        ),
    )(tokens, out_grad, expert_ids, combine, gate_weight[0], up_weight[0], down_t[0])
    return mixed, down_grad[None]


def weights_move(tokens, out_grad, expert_ids, combine, gate_weight, up_weight, down_t):
    experts = lax.axis_size("expert")
    tok_count, top_count = expert_ids.shape
    model_width = tokens.shape[1]
    slot_total = experts * CAP
    flat_ids = expert_ids.reshape(-1)
    onehot = (flat_ids[:, None] == jnp.arange(experts, dtype=jnp.int32)[None, :]).astype(jnp.int32)
    earlier = jnp.sum((jnp.cumsum(onehot, 0) - onehot) * onehot, 1)
    target = flat_ids * CAP + earlier
    sources = jnp.arange(tok_count * top_count, dtype=jnp.int32) // top_count
    slot_token = jnp.full((slot_total,), tok_count, jnp.int32).at[target].set(sources)
    slot_weight = jnp.zeros((slot_total,), jnp.float32).at[target].set(combine.reshape(-1))
    padded_rows = jnp.concatenate([tokens, jnp.zeros((1, model_width), jnp.bfloat16)], 0)
    padded_grad = jnp.concatenate([out_grad, jnp.zeros((1, model_width), jnp.bfloat16)], 0)
    send_rows = padded_rows[slot_token].reshape(experts, CAP, model_width)
    send_grad = (slot_weight[:, None] * padded_grad[slot_token].astype(jnp.float32)).astype(
        jnp.bfloat16
    )
    send_grad = send_grad.reshape(experts, CAP, model_width)
    recv_rows = lax.all_to_all(send_rows, "expert", split_axis=0, concat_axis=0, tiled=True)
    expert_rows = recv_rows.reshape(slot_total, model_width)
    gate_shard = gate_weight[0]
    up_shard = up_weight[0]
    down_shard = down_t[0]

    def add_rows(shard_piece):
        return jnp.dot(expert_rows, shard_piece, preferred_element_type=jnp.float32)

    gate_sum = add_rows(lax.all_gather(gate_shard, "dp", axis=0, tiled=True))
    up_sum = add_rows(lax.all_gather(up_shard, "dp", axis=0, tiled=True))
    hidden = (jax.nn.silu(gate_sum) * up_sum).astype(jnp.bfloat16)
    product = lax.dot_general(
        hidden,
        lax.all_gather(down_shard, "dp", axis=0, tiled=True),
        (((1,), (1,)), ((), ())),
        preferred_element_type=jnp.float32,
    )
    expert_out = product.astype(jnp.bfloat16)
    returned = lax.all_to_all(
        expert_out.reshape(experts, CAP, model_width),
        "expert",
        split_axis=0,
        concat_axis=0,
        tiled=True,
    )
    returned = returned.reshape(slot_total, model_width)[target]
    mixed = jnp.sum(
        returned.reshape(tok_count, top_count, model_width).astype(jnp.float32)
        * combine[:, :, None],
        1,
    )
    mixed = mixed.astype(jnp.bfloat16)
    recv_grad = lax.all_to_all(send_grad, "expert", split_axis=0, concat_axis=0, tiled=True)
    grad_rows = recv_grad.reshape(slot_total, model_width)
    own_grad = lax.psum_scatter(
        lax.dot_general(
            grad_rows, hidden, (((0,), (0,)), ((), ())), preferred_element_type=jnp.float32
        ).astype(jnp.bfloat16),
        "dp",
        scatter_dimension=0,
        tiled=True,
    )
    down_grad = own_grad[None]
    return (mixed, down_grad)


def solution(mesh):
    in_specs = (
        P(("group", "expert", "dp"), None),
        P(("group", "expert", "dp"), None),
        P(("group", "expert", "dp"), None),
        P(("group", "expert", "dp"), None),
        P("expert", "dp", None),
        P("expert", "dp", None),
        P("expert", "dp", None),
    )
    out_specs = (P(("group", "expert", "dp"), None), P(("group", "expert"), "dp", None))

    def per_device(*args):
        experts, replicas = lax.axis_size("expert"), lax.axis_size("dp")
        features, ff = args[0].shape[1], args[4].shape[2]
        slots = experts * replicas * CAP
        moved_tokens = slots * (3 * features // replicas + 3 * ff)
        moved_weights = 4 * features * ff + 3 * experts * CAP * features
        small = moved_tokens < moved_weights and slots <= 1024
        if small and replicas % 2 == 0 and features % (256 * replicas) == 0:
            return tokens_move(*args)
        return weights_move(*args)

    return jax.shard_map(
        per_device, mesh=mesh, in_specs=in_specs, out_specs=out_specs, check_vma=False
    )
```

```python
import functools

import jax
import jax.numpy as jnp
from jax import lax
from jax.experimental import pallas as pl
from jax.experimental.pallas import tpu as pltpu
from jax.sharding import PartitionSpec as P

CAP = 24
MESH = pl.DeviceIdType.MESH
F32 = jnp.float32
BF16 = jnp.bfloat16


def dot(a, b, dims=((1,), (0,))):
    return lax.dot_general(a, b, (dims, ((), ())), preferred_element_type=F32)


def kernel(
    experts,
    replicas,
    tokens_hbm,
    out_grad_hbm,
    ids_hbm,
    combine_hbm,
    gate_hbm,
    up_hbm,
    down_hbm,
    mixed,
    down_grad,
    gate_w,
    up_w,
    down_w,
    tokens,
    out_grad,
    expert_ids,
    combine,
    tok_send,
    tok_recv,
    grad_send,
    grad_recv,
    ret_send,
    ret_recv,
    mate_send,
    mate_recv,
    cross_send,
    cross_recv,
    own_sum,
    hid,
    load_sem,
    tok_ssem,
    tok_rsem,
    grad_ssem,
    grad_rsem,
    ret_ssem,
    ret_rsem,
    mate_ssem,
    mate_rsem,
    cross_ssem,
    cross_rsem,
    hid_ssem,
    hid_rsem,
    fwd_ssem,
    fwd_rsem,
):
    width = gate_hbm.shape[0]
    half = width // 2
    ff = gate_hbm.shape[1]
    rows = experts * CAP
    chips = replicas // 2
    e = lax.axis_index("expert")
    r = lax.axis_index("dp")
    chip = r // 2
    core = r % 2
    me = r * experts + e
    mate = {"dp": chip * 2 + 1 - core}

    loads = [
        pltpu.make_async_copy(src, dst, load_sem.at[i])
        for i, (src, dst) in enumerate(
            (
                (ids_hbm, expert_ids),
                (tokens_hbm, tokens),
                (combine_hbm, combine),
                (out_grad_hbm, out_grad),
                (gate_hbm, gate_w),
                (up_hbm, up_w),
                (down_hbm, down_w),
            )
        )
    ]
    for load in loads:
        load.start()

    peers = []
    for dr in range(replicas):
        for de in range(experts):
            if dr or de:
                pe, pr = lax.rem(e + de, experts), lax.rem(r + dr, replicas)
                peers.append((pe, pr, pr * experts + pe))
    barrier = pltpu.get_barrier_semaphore()
    for pe, pr, _ in peers:
        pl.semaphore_signal(barrier, inc=1, device_id={"expert": pe, "dp": pr}, device_id_type=MESH)

    def exchange(src, dst, ssem, rsem):
        copies = []
        for pe, pr, n in peers:
            copies.append(
                (
                    pltpu.make_async_remote_copy(
                        src_ref=src.at[n],
                        dst_ref=dst.at[me],
                        send_sem=ssem.at[n],
                        recv_sem=rsem.at[me],
                        device_id={"expert": pe, "dp": pr},
                        device_id_type=MESH,
                    ),
                    pltpu.make_async_remote_copy(
                        src_ref=src.at[n],
                        dst_ref=dst.at[n],
                        send_sem=ssem.at[n],
                        recv_sem=rsem.at[n],
                        device_id={"expert": pe, "dp": pr},
                        device_id_type=MESH,
                    ),
                )
            )
        return copies

    def slab(block):
        return jnp.concatenate([block[:, :half], block[:, half:]], 0).astype(BF16)

    def fill(dst, value):
        for pr in range(replicas):
            for pe in range(experts):
                dst[pr * experts + pe] = slab(
                    value[pe * CAP : (pe + 1) * CAP, pr * width : (pr + 1) * width]
                )

    tok_count = tokens.shape[0]
    top = expert_ids.shape[0]
    line = lax.broadcasted_iota(jnp.int32, (rows, tok_count), 0)
    owner = jnp.zeros((rows, tok_count), jnp.int32)
    for j in range(1, experts):
        owner = owner + (line >= j * CAP).astype(jnp.int32)
    place = (line - owner * CAP).astype(F32)
    token_down = lax.broadcasted_iota(jnp.int32, (tok_count, tok_count), 0)
    token_along = lax.broadcasted_iota(jnp.int32, (tok_count, tok_count), 1)
    earlier = (token_down < token_along).astype(F32).astype(BF16)
    loads[0].wait()
    picks = [(expert_ids[k : k + 1, :] == owner).astype(F32) for k in range(top)]
    named = functools.reduce(jnp.add, picks)
    here = jnp.where(dot(named.astype(BF16), earlier) == place, 1.0, 0.0)
    picks = [pick * here for pick in picks]
    either = (named * here).astype(BF16)
    loads[1].wait()
    fill(tok_send, dot(either, tokens[...]))
    pl.semaphore_wait(barrier, len(peers))

    tok_copies = exchange(tok_send, tok_recv, tok_ssem, tok_rsem)
    for out, _ in tok_copies:
        out.start()
    tok_recv[pl.ds(me, 1)] = tok_send[pl.ds(me, 1)]
    loads[2].wait()
    loads[3].wait()
    slot_weight = jnp.zeros((rows, 1), F32)
    weights = []
    for k in range(top):
        row = combine[k : k + 1, :]
        slot_weight = slot_weight + jnp.sum(picks[k] * row, 1, keepdims=True)
        weights.append(jnp.sum(jnp.where(token_down == token_along, row, 0.0), 1, keepdims=True))
    fill(grad_send, slot_weight * dot(either, out_grad[...]))
    picks = [pick.astype(BF16) for pick in picks]
    grad_recv[pl.ds(me, 1)] = grad_send[pl.ds(me, 1)]
    for load in loads[4:6]:
        load.wait()
    for out, back in tok_copies:
        back.wait_recv()
    grad_copies = exchange(grad_send, grad_recv, grad_ssem, grad_rsem)
    for out, _ in grad_copies:
        out.start()

    def mate_copy(c):
        return pltpu.make_async_remote_copy(
            src_ref=mate_send.at[c],
            dst_ref=mate_recv.at[c],
            send_sem=mate_ssem.at[c],
            recv_sem=mate_rsem.at[c],
            device_id=mate,
            device_id_type=MESH,
        )

    pair = 2 * experts
    other_chips = [lax.rem(chip + d, chips) for d in range(1, chips)]
    for d in list(range(1, chips)) + [0]:
        c = lax.rem(chip + d, chips)
        for j in range(2):
            at = pl.ds((c * 2 + j) * experts, experts)
            x = tok_recv[at]
            lo, hi = x[:, :CAP].reshape(rows, half), x[:, CAP:].reshape(rows, half)
            for i, w in enumerate((gate_w, up_w)):
                part = dot(lo, w[:half]) + dot(hi, w[half:])

                @pl.when(core == j)
                def _():
                    own_sum[d, i] = part

                @pl.when(core != j)
                def _():
                    mate_send[d, i] = part.astype(BF16)

        mate_copy(d).start()

    def cross_copy(d):
        return pltpu.make_async_remote_copy(
            src_ref=cross_send.at[d],
            dst_ref=cross_recv.at[d],
            send_sem=cross_ssem.at[d],
            recv_sem=cross_rsem.at[d],
            device_id={"dp": lax.rem(chip + d, chips) * 2 + core},
            device_id_type=MESH,
        )

    for d in range(1, chips):
        mate_copy(d).wait_recv()
        cross_send[d] = (own_sum[d] + mate_recv[d].astype(F32)).astype(BF16)
        cross_copy(d).start()
    mate_copy(0).wait_recv()
    total = own_sum[0] + mate_recv[0].astype(F32)
    own_sum[0] = total
    for d in range(1, chips):
        cross_copy(d).wait_recv()
    total = own_sum[0]
    for d in range(1, chips):
        total = total + cross_recv[d].astype(F32)
    gate, up = total[0], total[1]
    hid[pl.ds(r, 1)] = ((gate / (1.0 + jnp.exp(-gate))) * up).astype(BF16)[None]

    def hid_copy(d, src, at, target, ssem, rsem):
        return pltpu.make_async_remote_copy(
            src_ref=hid.at[src],
            dst_ref=hid.at[at],
            send_sem=ssem.at[d],
            recv_sem=rsem.at[d],
            device_id={"dp": target},
            device_id_type=MESH,
        )

    hid_out, hid_in = [], []
    for d in range(1, chips):
        ahead = lax.rem(chip + d, chips) * 2 + core
        behind = lax.rem(chip + chips - d, chips) * 2 + core
        hid_out.append(hid_copy(d, r, r, ahead, hid_ssem, hid_rsem))
        hid_in.append(hid_copy(d, r, behind, ahead, hid_ssem, hid_rsem))
    for copy in hid_out:
        copy.start()
    mate_r = chip * 2 + 1 - core
    mate_out = hid_copy(0, r, r, mate_r, fwd_ssem, fwd_rsem)
    mate_in = hid_copy(0, r, mate_r, mate_r, fwd_ssem, fwd_rsem)
    mate_out.start()
    loads[6].wait()

    ret_copies = exchange(ret_send, ret_recv, ret_ssem, ret_rsem)

    def give_back(pr):
        out = dot(hid[pr], down_w[...], ((1,), (1,)))
        for pe in range(experts):
            ret_send[pr * experts + pe] = slab(out[pe * CAP : (pe + 1) * CAP])

    def send_back(dr_pr, skip_self):
        for de in range(experts):
            if skip_self and de == 0:
                continue
            pe = lax.rem(e + de, experts)
            n = dr_pr * experts + pe
            pltpu.make_async_remote_copy(
                src_ref=ret_send.at[n],
                dst_ref=ret_recv.at[me],
                send_sem=ret_ssem.at[n],
                recv_sem=ret_rsem.at[me],
                device_id={"expert": pe, "dp": dr_pr},
                device_id_type=MESH,
            ).start()

    give_back(r)
    send_back(r, True)
    ret_recv[pl.ds(me, 1)] = ret_send[pl.ds(me, 1)]
    mate_in.wait_recv()
    give_back(mate_r)
    send_back(mate_r, False)
    forwards = []
    for d in range(1, chips):
        hid_in[d - 1].wait_recv()
        behind = lax.rem(chip + chips - d, chips)
        out = hid_copy(d, behind * 2 + core, behind * 2 + core, mate_r, fwd_ssem, fwd_rsem)
        into = hid_copy(d, behind * 2 + core, behind * 2 + 1 - core, mate_r, fwd_ssem, fwd_rsem)
        out.start()
        forwards.append((out, into))
        give_back(behind * 2 + core)
        send_back(behind * 2 + core, False)
    for d in range(1, chips):
        forwards[d - 1][1].wait_recv()
        behind = lax.rem(chip + chips - d, chips)
        give_back(behind * 2 + 1 - core)
        send_back(behind * 2 + 1 - core, False)

    for _, back in grad_copies:
        back.wait_recv()
    hidden = hid[...].reshape(replicas * rows, ff)
    for h in range(2):
        g = grad_recv[:, h * CAP : (h + 1) * CAP].reshape(replicas * rows, half)
        down_grad[h * half : (h + 1) * half] = dot(g, hidden, ((0,), (0,))).astype(BF16)

    for _, back in ret_copies:
        back.wait_recv()
    for pr in range(replicas):
        for h in range(2):
            block = ret_recv[pr * experts : (pr + 1) * experts, h * CAP : (h + 1) * CAP]
            block = block.reshape(rows, half)
            value = weights[0] * dot(picks[0], block, ((0,), (0,)))
            for k in range(1, top):
                value = value + weights[k] * dot(picks[k], block, ((0,), (0,)))
            start = pr * width + h * half
            mixed[:, start : start + half] = value.astype(BF16)

    for copies in (tok_copies, grad_copies, ret_copies):
        for out, _ in copies:
            out.wait_send()
    for d in range(chips):
        mate_copy(d).wait_send()
    for d in range(1, chips):
        cross_copy(d).wait_send()
    for copy in hid_out:
        copy.wait_send()
    mate_out.wait_send()
    for out, _ in forwards:
        out.wait_send()


def tokens_move(tokens, out_grad, expert_ids, combine, gate_weight, up_weight, down_t):
    experts, replicas = lax.axis_size("expert"), lax.axis_size("dp")
    _, width, ff = gate_weight.shape
    top = expert_ids.shape[1]
    peers, chips, rows = experts * replicas, replicas // 2, experts * CAP
    slabs = pltpu.VMEM((peers, 2 * CAP, width // 2), BF16)
    dma = pltpu.SemaphoreType.DMA
    vmem = pl.BlockSpec(memory_space=pltpu.VMEM)
    hbm = pl.BlockSpec(memory_space=pl.ANY)
    mixed, down_grad = pl.pallas_call(
        functools.partial(kernel, experts, replicas),
        out_shape=(
            jax.ShapeDtypeStruct(tokens.shape, BF16),
            jax.ShapeDtypeStruct((width, ff), BF16),
        ),
        in_specs=[hbm] * 7,
        out_specs=(vmem, vmem),
        scratch_shapes=[pltpu.VMEM((width, ff), BF16)] * 3
        + [pltpu.VMEM(tokens.shape, BF16)] * 2
        + [pltpu.VMEM((top, tokens.shape[0]), jnp.int32)]
        + [pltpu.VMEM((top, tokens.shape[0]), F32)]
        + [slabs] * 6
        + [pltpu.VMEM((chips, 2, rows, ff), BF16)] * 4
        + [pltpu.VMEM((chips, 2, rows, ff), F32), pltpu.VMEM((replicas, rows, ff), BF16)]
        + [dma((7,))]
        + [dma((peers,))] * 6
        + [dma((chips,))] * 8,
        compiler_params=pltpu.CompilerParams(
            collective_id=0, has_side_effects=True, vmem_limit_bytes=60 * 1024 * 1024
        ),
    )(tokens, out_grad, expert_ids.T, combine.T, gate_weight[0], up_weight[0], down_t[0])
    return mixed, down_grad[None]


def weights_move(tokens, out_grad, expert_ids, combine, gate_weight, up_weight, down_t):
    experts = lax.axis_size("expert")
    tok_count, top_count = expert_ids.shape
    model_width = tokens.shape[1]
    slot_total = experts * CAP
    flat_ids = expert_ids.reshape(-1)
    onehot = (flat_ids[:, None] == jnp.arange(experts, dtype=jnp.int32)[None, :]).astype(jnp.int32)
    earlier = jnp.sum((jnp.cumsum(onehot, 0) - onehot) * onehot, 1)
    target = flat_ids * CAP + earlier
    sources = jnp.arange(tok_count * top_count, dtype=jnp.int32) // top_count
    slot_token = jnp.full((slot_total,), tok_count, jnp.int32).at[target].set(sources)
    slot_weight = jnp.zeros((slot_total,), jnp.float32).at[target].set(combine.reshape(-1))
    padded_rows = jnp.concatenate([tokens, jnp.zeros((1, model_width), jnp.bfloat16)], 0)
    padded_grad = jnp.concatenate([out_grad, jnp.zeros((1, model_width), jnp.bfloat16)], 0)
    send_rows = padded_rows[slot_token].reshape(experts, CAP, model_width)
    send_grad = (slot_weight[:, None] * padded_grad[slot_token].astype(jnp.float32)).astype(
        jnp.bfloat16
    )
    send_grad = send_grad.reshape(experts, CAP, model_width)
    recv_rows = lax.all_to_all(send_rows, "expert", split_axis=0, concat_axis=0, tiled=True)
    expert_rows = recv_rows.reshape(slot_total, model_width)
    gate_shard = gate_weight[0]
    up_shard = up_weight[0]
    down_shard = down_t[0]

    def add_rows(shard_piece):
        return jnp.dot(expert_rows, shard_piece, preferred_element_type=jnp.float32)

    gate_sum = add_rows(lax.all_gather(gate_shard, "dp", axis=0, tiled=True))
    up_sum = add_rows(lax.all_gather(up_shard, "dp", axis=0, tiled=True))
    hidden = (jax.nn.silu(gate_sum) * up_sum).astype(jnp.bfloat16)
    product = lax.dot_general(
        hidden,
        lax.all_gather(down_shard, "dp", axis=0, tiled=True),
        (((1,), (1,)), ((), ())),
        preferred_element_type=jnp.float32,
    )
    expert_out = product.astype(jnp.bfloat16)
    returned = lax.all_to_all(
        expert_out.reshape(experts, CAP, model_width),
        "expert",
        split_axis=0,
        concat_axis=0,
        tiled=True,
    )
    returned = returned.reshape(slot_total, model_width)[target]
    mixed = jnp.sum(
        returned.reshape(tok_count, top_count, model_width).astype(jnp.float32)
        * combine[:, :, None],
        1,
    )
    mixed = mixed.astype(jnp.bfloat16)
    recv_grad = lax.all_to_all(send_grad, "expert", split_axis=0, concat_axis=0, tiled=True)
    grad_rows = recv_grad.reshape(slot_total, model_width)
    own_grad = lax.psum_scatter(
        lax.dot_general(
            grad_rows, hidden, (((0,), (0,)), ((), ())), preferred_element_type=jnp.float32
        ).astype(jnp.bfloat16),
        "dp",
        scatter_dimension=0,
        tiled=True,
    )
    down_grad = own_grad[None]
    return (mixed, down_grad)


def solution(mesh):
    in_specs = (
        P(("group", "expert", "dp"), None),
        P(("group", "expert", "dp"), None),
        P(("group", "expert", "dp"), None),
        P(("group", "expert", "dp"), None),
        P("expert", "dp", None),
        P("expert", "dp", None),
        P("expert", "dp", None),
    )
    out_specs = (P(("group", "expert", "dp"), None), P(("group", "expert"), "dp", None))

    def per_device(*args):
        experts, replicas = lax.axis_size("expert"), lax.axis_size("dp")
        features, ff = args[0].shape[1], args[4].shape[2]
        slots = experts * replicas * CAP
        moved_tokens = slots * (3 * features // replicas + 3 * ff)
        moved_weights = 4 * features * ff + 3 * experts * CAP * features
        small = moved_tokens < moved_weights and slots <= 1024
        if small and replicas % 2 == 0 and features % (256 * replicas) == 0:
            return tokens_move(*args)
        return weights_move(*args)

    return jax.shard_map(
        per_device, mesh=mesh, in_specs=in_specs, out_specs=out_specs, check_vma=False
    )
```

```python
import functools

import jax
import jax.numpy as jnp
from jax import lax
from jax.experimental import pallas as pl
from jax.experimental.pallas import tpu as pltpu
from jax.sharding import PartitionSpec as P

CAP = 24
MESH = pl.DeviceIdType.MESH
F32 = jnp.float32
BF16 = jnp.bfloat16


def dot(a, b, dims=((1,), (0,))):
    return lax.dot_general(a, b, (dims, ((), ())), preferred_element_type=F32)


def kernel(
    experts,
    replicas,
    tokens_hbm,
    out_grad_hbm,
    ids_hbm,
    combine_hbm,
    gate_hbm,
    up_hbm,
    down_hbm,
    mixed_hbm,
    down_grad_hbm,
    gate_w,
    up_w,
    down_w,
    tokens,
    out_grad,
    expert_ids,
    combine,
    mixed,
    down_grad,
    tok_send,
    tok_recv,
    grad_send,
    grad_recv,
    ret_send,
    ret_recv,
    mate_send,
    mate_recv,
    cross_send,
    cross_recv,
    own_sum,
    hid,
    load_sem,
    store_sem,
    tok_ssem,
    tok_rsem,
    grad_ssem,
    grad_rsem,
    ret_ssem,
    ret_rsem,
    mate_ssem,
    mate_rsem,
    cross_ssem,
    cross_rsem,
    hid_ssem,
    hid_rsem,
    fwd_ssem,
    fwd_rsem,
):
    width = gate_hbm.shape[0]
    half = width // 2
    ff = gate_hbm.shape[1]
    rows = experts * CAP
    chips = replicas // 2
    e = lax.axis_index("expert")
    r = lax.axis_index("dp")
    chip = r // 2
    core = r % 2
    me = r * experts + e
    mate = {"dp": chip * 2 + 1 - core}

    loads = [
        pltpu.make_async_copy(src, dst, load_sem.at[i])
        for i, (src, dst) in enumerate(
            (
                (ids_hbm, expert_ids),
                (tokens_hbm, tokens),
                (combine_hbm, combine),
                (out_grad_hbm, out_grad),
                (gate_hbm, gate_w),
                (up_hbm, up_w),
                (down_hbm, down_w),
            )
        )
    ]
    for load in loads:
        load.start()

    peers, chip_peers = [], {}
    for d in list(range(1, chips)) + [0]:
        chip_peers[d] = []
        for dc in range(2):
            for de in range(experts):
                if d or dc or de:
                    pe = lax.rem(e + de, experts)
                    pr = lax.rem(chip + d, chips) * 2 + lax.rem(core + dc, 2)
                    chip_peers[d].append(len(peers))
                    peers.append((pe, pr, pr * experts + pe))
    barrier = pltpu.get_barrier_semaphore()
    for pe, pr, _ in peers:
        pl.semaphore_signal(barrier, inc=1, device_id={"expert": pe, "dp": pr}, device_id_type=MESH)

    def exchange(src, dst, ssem, rsem):
        copies = []
        for pe, pr, n in peers:
            copies.append(
                (
                    pltpu.make_async_remote_copy(
                        src_ref=src.at[n],
                        dst_ref=dst.at[me],
                        send_sem=ssem.at[n],
                        recv_sem=rsem.at[me],
                        device_id={"expert": pe, "dp": pr},
                        device_id_type=MESH,
                    ),
                    pltpu.make_async_remote_copy(
                        src_ref=src.at[n],
                        dst_ref=dst.at[n],
                        send_sem=ssem.at[n],
                        recv_sem=rsem.at[n],
                        device_id={"expert": pe, "dp": pr},
                        device_id_type=MESH,
                    ),
                )
            )
        return copies

    def slab(block):
        return jnp.concatenate([block[:, :half], block[:, half:]], 0).astype(BF16)

    def fill(dst, value):
        for pr in range(replicas):
            for pe in range(experts):
                dst[pr * experts + pe] = slab(
                    value[pe * CAP : (pe + 1) * CAP, pr * width : (pr + 1) * width]
                )

    tok_count = tokens.shape[0]
    top = expert_ids.shape[0]
    line = lax.broadcasted_iota(jnp.int32, (rows, tok_count), 0)
    owner = jnp.zeros((rows, tok_count), jnp.int32)
    for j in range(1, experts):
        owner = owner + (line >= j * CAP).astype(jnp.int32)
    place = (line - owner * CAP).astype(F32)
    token_down = lax.broadcasted_iota(jnp.int32, (tok_count, tok_count), 0)
    token_along = lax.broadcasted_iota(jnp.int32, (tok_count, tok_count), 1)
    earlier = (token_down < token_along).astype(F32).astype(BF16)
    loads[0].wait()
    picks = [(expert_ids[k : k + 1, :] == owner).astype(F32) for k in range(top)]
    named = functools.reduce(jnp.add, picks)
    here = jnp.where(dot(named.astype(BF16), earlier) == place, 1.0, 0.0)
    picks = [pick * here for pick in picks]
    either = (named * here).astype(BF16)
    loads[1].wait()
    fill(tok_send, dot(either, tokens[...]))
    pl.semaphore_wait(barrier, len(peers))

    tok_copies = exchange(tok_send, tok_recv, tok_ssem, tok_rsem)
    for out, _ in tok_copies:
        out.start()
    tok_recv[pl.ds(me, 1)] = tok_send[pl.ds(me, 1)]
    loads[2].wait()
    loads[3].wait()
    slot_weight = jnp.zeros((rows, 1), F32)
    weights = []
    for k in range(top):
        row = combine[k : k + 1, :]
        slot_weight = slot_weight + jnp.sum(picks[k] * row, 1, keepdims=True)
        weights.append(jnp.sum(jnp.where(token_down == token_along, row, 0.0), 1, keepdims=True))
    fill(grad_send, slot_weight * dot(either, out_grad[...]))
    picks = [pick.astype(BF16) for pick in picks]
    grad_recv[pl.ds(me, 1)] = grad_send[pl.ds(me, 1)]
    for load in loads[4:6]:
        load.wait()
    grad_copies = exchange(grad_send, grad_recv, grad_ssem, grad_rsem)

    def mate_copy(c):
        return pltpu.make_async_remote_copy(
            src_ref=mate_send.at[c],
            dst_ref=mate_recv.at[c],
            send_sem=mate_ssem.at[c],
            recv_sem=mate_rsem.at[c],
            device_id=mate,
            device_id_type=MESH,
        )

    def cross_copy(d):
        return pltpu.make_async_remote_copy(
            src_ref=cross_send.at[d],
            dst_ref=cross_recv.at[d],
            send_sem=cross_ssem.at[d],
            recv_sem=cross_rsem.at[d],
            device_id={"dp": lax.rem(chip + d, chips) * 2 + core},
            device_id_type=MESH,
        )

    for d in list(range(1, chips)) + [0]:
        for i in chip_peers[d]:
            tok_copies[i][1].wait_recv()
        if d == 0:
            for out, _ in grad_copies:
                out.start()
        at = pl.ds(lax.rem(chip + d, chips) * 2 * experts, 2 * experts)
        x = tok_recv[at]
        lo, hi = x[:, :CAP].reshape(2 * rows, half), x[:, CAP:].reshape(2 * rows, half)
        for i, w in enumerate((gate_w, up_w)):
            part = dot(lo, w[:half]) + dot(hi, w[half:])
            for j in range(2):
                share = part[j * rows : (j + 1) * rows]

                @pl.when(core == j)
                def _():
                    own_sum[d, i] = share

                @pl.when(core != j)
                def _():
                    mate_send[d, i] = share.astype(BF16)

        mate_copy(d).start()
        mate_copy(d).wait_recv()
        if d:
            cross_send[d] = (own_sum[d] + mate_recv[d].astype(F32)).astype(BF16)
            cross_copy(d).start()
        else:
            own_sum[0] = own_sum[0] + mate_recv[0].astype(F32)
    for d in range(1, chips):
        cross_copy(d).wait_recv()
    total = own_sum[0]
    for d in range(1, chips):
        total = total + cross_recv[d].astype(F32)
    gate, up = total[0], total[1]
    hid[pl.ds(r, 1)] = ((gate / (1.0 + jnp.exp(-gate))) * up).astype(BF16)[None]

    def hid_copy(d, src, at, target, ssem, rsem):
        return pltpu.make_async_remote_copy(
            src_ref=hid.at[src],
            dst_ref=hid.at[at],
            send_sem=ssem.at[d],
            recv_sem=rsem.at[d],
            device_id={"dp": target},
            device_id_type=MESH,
        )

    hid_out, hid_in = [], []
    for d in range(1, chips):
        ahead = lax.rem(chip + d, chips) * 2 + core
        behind = lax.rem(chip + chips - d, chips) * 2 + core
        hid_out.append(hid_copy(d, r, r, ahead, hid_ssem, hid_rsem))
        hid_in.append(hid_copy(d, r, behind, ahead, hid_ssem, hid_rsem))
    for copy in hid_out:
        copy.start()
    mate_r = chip * 2 + 1 - core
    mate_out = hid_copy(0, r, r, mate_r, fwd_ssem, fwd_rsem)
    mate_in = hid_copy(0, r, mate_r, mate_r, fwd_ssem, fwd_rsem)
    mate_out.start()
    loads[6].wait()

    ret_copies = exchange(ret_send, ret_recv, ret_ssem, ret_rsem)

    def give_back(pr):
        out = dot(hid[pr], down_w[...], ((1,), (1,)))
        for pe in range(experts):
            ret_send[pr * experts + pe] = slab(out[pe * CAP : (pe + 1) * CAP])

    def send_back(dr_pr, skip_self):
        for de in range(experts):
            if skip_self and de == 0:
                continue
            pe = lax.rem(e + de, experts)
            n = dr_pr * experts + pe
            pltpu.make_async_remote_copy(
                src_ref=ret_send.at[n],
                dst_ref=ret_recv.at[me],
                send_sem=ret_ssem.at[n],
                recv_sem=ret_rsem.at[me],
                device_id={"expert": pe, "dp": dr_pr},
                device_id_type=MESH,
            ).start()

    give_back(r)
    send_back(r, True)
    ret_recv[pl.ds(me, 1)] = ret_send[pl.ds(me, 1)]
    mate_in.wait_recv()
    give_back(mate_r)
    send_back(mate_r, False)
    forwards = []
    for d in range(1, chips):
        hid_in[d - 1].wait_recv()
        behind = lax.rem(chip + chips - d, chips)
        out = hid_copy(d, behind * 2 + core, behind * 2 + core, mate_r, fwd_ssem, fwd_rsem)
        into = hid_copy(d, behind * 2 + core, behind * 2 + 1 - core, mate_r, fwd_ssem, fwd_rsem)
        out.start()
        forwards.append((out, into))
        give_back(behind * 2 + core)
        send_back(behind * 2 + core, False)
    for d in range(1, chips):
        forwards[d - 1][1].wait_recv()
        behind = lax.rem(chip + chips - d, chips)
        give_back(behind * 2 + 1 - core)
        send_back(behind * 2 + 1 - core, False)

    for _, back in grad_copies:
        back.wait_recv()
    hidden = hid[...].reshape(replicas * rows, ff)
    for h in range(2):
        g = grad_recv[:, h * CAP : (h + 1) * CAP].reshape(replicas * rows, half)
        down_grad[h * half : (h + 1) * half] = dot(g, hidden, ((0,), (0,))).astype(BF16)

    store_grad = pltpu.make_async_copy(down_grad, down_grad_hbm, store_sem.at[0])
    store_grad.start()
    for _, back in ret_copies:
        back.wait_recv()
    for pr in range(replicas):
        for h in range(2):
            block = ret_recv[pr * experts : (pr + 1) * experts, h * CAP : (h + 1) * CAP]
            block = block.reshape(rows, half)
            value = weights[0] * dot(picks[0], block, ((0,), (0,)))
            for k in range(1, top):
                value = value + weights[k] * dot(picks[k], block, ((0,), (0,)))
            start = pr * width + h * half
            mixed[:, start : start + half] = value.astype(BF16)

    store_mixed = pltpu.make_async_copy(mixed, mixed_hbm, store_sem.at[1])
    store_mixed.start()
    for copies in (tok_copies, grad_copies, ret_copies):
        for out, _ in copies:
            out.wait_send()
    for d in range(chips):
        mate_copy(d).wait_send()
    for d in range(1, chips):
        cross_copy(d).wait_send()
    for copy in hid_out:
        copy.wait_send()
    mate_out.wait_send()
    for out, _ in forwards:
        out.wait_send()
    store_grad.wait()
    store_mixed.wait()


def tokens_move(tokens, out_grad, expert_ids, combine, gate_weight, up_weight, down_t):
    experts, replicas = lax.axis_size("expert"), lax.axis_size("dp")
    _, width, ff = gate_weight.shape
    top = expert_ids.shape[1]
    peers, chips, rows = experts * replicas, replicas // 2, experts * CAP
    slabs = pltpu.VMEM((peers, 2 * CAP, width // 2), BF16)
    dma = pltpu.SemaphoreType.DMA
    hbm = pl.BlockSpec(memory_space=pl.ANY)
    mixed, down_grad = pl.pallas_call(
        functools.partial(kernel, experts, replicas),
        out_shape=(
            jax.ShapeDtypeStruct(tokens.shape, BF16),
            jax.ShapeDtypeStruct((width, ff), BF16),
        ),
        in_specs=[hbm] * 7,
        out_specs=(hbm, hbm),
        scratch_shapes=[pltpu.VMEM((width, ff), BF16)] * 3
        + [pltpu.VMEM(tokens.shape, BF16)] * 2
        + [pltpu.VMEM((top, tokens.shape[0]), jnp.int32)]
        + [pltpu.VMEM((top, tokens.shape[0]), F32)]
        + [pltpu.VMEM(tokens.shape, BF16), pltpu.VMEM((width, ff), BF16)]
        + [slabs] * 6
        + [pltpu.VMEM((chips, 2, rows, ff), BF16)] * 4
        + [pltpu.VMEM((chips, 2, rows, ff), F32), pltpu.VMEM((replicas, rows, ff), BF16)]
        + [dma((7,)), dma((2,))]
        + [dma((peers,))] * 6
        + [dma((chips,))] * 8,
        compiler_params=pltpu.CompilerParams(
            collective_id=0, has_side_effects=True, vmem_limit_bytes=60 * 1024 * 1024
        ),
    )(tokens, out_grad, expert_ids.T, combine.T, gate_weight[0], up_weight[0], down_t[0])
    return mixed, down_grad[None]


def weights_move(tokens, out_grad, expert_ids, combine, gate_weight, up_weight, down_t):
    experts = lax.axis_size("expert")
    tok_count, top_count = expert_ids.shape
    model_width = tokens.shape[1]
    slot_total = experts * CAP
    flat_ids = expert_ids.reshape(-1)
    onehot = (flat_ids[:, None] == jnp.arange(experts, dtype=jnp.int32)[None, :]).astype(jnp.int32)
    earlier = jnp.sum((jnp.cumsum(onehot, 0) - onehot) * onehot, 1)
    target = flat_ids * CAP + earlier
    sources = jnp.arange(tok_count * top_count, dtype=jnp.int32) // top_count
    slot_token = jnp.full((slot_total,), tok_count, jnp.int32).at[target].set(sources)
    slot_weight = jnp.zeros((slot_total,), jnp.float32).at[target].set(combine.reshape(-1))
    padded_rows = jnp.concatenate([tokens, jnp.zeros((1, model_width), jnp.bfloat16)], 0)
    padded_grad = jnp.concatenate([out_grad, jnp.zeros((1, model_width), jnp.bfloat16)], 0)
    send_rows = padded_rows[slot_token].reshape(experts, CAP, model_width)
    send_grad = (slot_weight[:, None] * padded_grad[slot_token].astype(jnp.float32)).astype(
        jnp.bfloat16
    )
    send_grad = send_grad.reshape(experts, CAP, model_width)
    recv_rows = lax.all_to_all(send_rows, "expert", split_axis=0, concat_axis=0, tiled=True)
    expert_rows = recv_rows.reshape(slot_total, model_width)
    gate_shard = gate_weight[0]
    up_shard = up_weight[0]
    down_shard = down_t[0]

    def add_rows(shard_piece):
        return jnp.dot(expert_rows, shard_piece, preferred_element_type=jnp.float32)

    gate_sum = add_rows(lax.all_gather(gate_shard, "dp", axis=0, tiled=True))
    up_sum = add_rows(lax.all_gather(up_shard, "dp", axis=0, tiled=True))
    hidden = (jax.nn.silu(gate_sum) * up_sum).astype(jnp.bfloat16)
    product = lax.dot_general(
        hidden,
        lax.all_gather(down_shard, "dp", axis=0, tiled=True),
        (((1,), (1,)), ((), ())),
        preferred_element_type=jnp.float32,
    )
    expert_out = product.astype(jnp.bfloat16)
    returned = lax.all_to_all(
        expert_out.reshape(experts, CAP, model_width),
        "expert",
        split_axis=0,
        concat_axis=0,
        tiled=True,
    )
    returned = returned.reshape(slot_total, model_width)[target]
    mixed = jnp.sum(
        returned.reshape(tok_count, top_count, model_width).astype(jnp.float32)
        * combine[:, :, None],
        1,
    )
    mixed = mixed.astype(jnp.bfloat16)
    recv_grad = lax.all_to_all(send_grad, "expert", split_axis=0, concat_axis=0, tiled=True)
    grad_rows = recv_grad.reshape(slot_total, model_width)
    own_grad = lax.psum_scatter(
        lax.dot_general(
            grad_rows, hidden, (((0,), (0,)), ((), ())), preferred_element_type=jnp.float32
        ).astype(jnp.bfloat16),
        "dp",
        scatter_dimension=0,
        tiled=True,
    )
    down_grad = own_grad[None]
    return (mixed, down_grad)


def solution(mesh):
    in_specs = (
        P(("group", "expert", "dp"), None),
        P(("group", "expert", "dp"), None),
        P(("group", "expert", "dp"), None),
        P(("group", "expert", "dp"), None),
        P("expert", "dp", None),
        P("expert", "dp", None),
        P("expert", "dp", None),
    )
    out_specs = (P(("group", "expert", "dp"), None), P(("group", "expert"), "dp", None))

    def per_device(*args):
        experts, replicas = lax.axis_size("expert"), lax.axis_size("dp")
        features, ff = args[0].shape[1], args[4].shape[2]
        slots = experts * replicas * CAP
        moved_tokens = slots * (3 * features // replicas + 3 * ff)
        moved_weights = 4 * features * ff + 3 * experts * CAP * features
        small = moved_tokens < moved_weights and slots <= 1024
        if small and replicas % 2 == 0 and features % (256 * replicas) == 0:
            return tokens_move(*args)
        return weights_move(*args)

    return jax.shard_map(
        per_device, mesh=mesh, in_specs=in_specs, out_specs=out_specs, check_vma=False
    )
```

```python
import functools

import jax
import jax.numpy as jnp
from jax import lax
from jax.experimental import pallas as pl
from jax.experimental.pallas import tpu as pltpu
from jax.sharding import PartitionSpec as P

CAP = 24
MESH = pl.DeviceIdType.MESH
F32 = jnp.float32
BF16 = jnp.bfloat16


def dot(a, b, dims=((1,), (0,))):
    return lax.dot_general(a, b, (dims, ((), ())), preferred_element_type=F32)


def kernel(
    experts,
    replicas,
    tokens_hbm,
    out_grad_hbm,
    ids_hbm,
    combine_hbm,
    gate_hbm,
    up_hbm,
    down_hbm,
    mixed_hbm,
    down_grad_hbm,
    gate_w,
    up_w,
    down_w,
    tokens,
    out_grad,
    expert_ids,
    combine,
    mixed,
    down_grad,
    tok_send,
    tok_recv,
    grad_send,
    grad_recv,
    ret_send,
    ret_recv,
    mate_send,
    mate_recv,
    cross_send,
    cross_recv,
    own_sum,
    hid,
    load_sem,
    store_sem,
    tok_ssem,
    tok_rsem,
    grad_ssem,
    grad_rsem,
    ret_ssem,
    ret_rsem,
    mate_ssem,
    mate_rsem,
    cross_ssem,
    cross_rsem,
    hid_ssem,
    hid_rsem,
    fwd_ssem,
    fwd_rsem,
):
    width = gate_hbm.shape[0]
    half = width // 2
    ff = gate_hbm.shape[1]
    rows = experts * CAP
    chips = replicas // 2
    e = lax.axis_index("expert")
    r = lax.axis_index("dp")
    chip = r // 2
    core = r % 2
    me = r * experts + e
    mate = {"dp": chip * 2 + 1 - core}

    loads = [
        pltpu.make_async_copy(src, dst, load_sem.at[i])
        for i, (src, dst) in enumerate(
            (
                (ids_hbm, expert_ids),
                (tokens_hbm, tokens),
                (combine_hbm, combine),
                (out_grad_hbm, out_grad),
                (gate_hbm, gate_w),
                (up_hbm, up_w),
                (down_hbm, down_w),
            )
        )
    ]
    for load in loads:
        load.start()

    peers, chip_peers = [], {}
    for d in list(range(1, chips)) + [0]:
        chip_peers[d] = []
        for dc in range(2):
            for de in range(experts):
                if d or dc or de:
                    pe = lax.rem(e + de, experts)
                    pr = lax.rem(chip + d, chips) * 2 + lax.rem(core + dc, 2)
                    chip_peers[d].append(len(peers))
                    peers.append((pe, pr, pr * experts + pe))
    barrier = pltpu.get_barrier_semaphore()
    for pe, pr, _ in peers:
        pl.semaphore_signal(barrier, inc=1, device_id={"expert": pe, "dp": pr}, device_id_type=MESH)

    def exchange(src, dst, ssem, rsem):
        copies = []
        for pe, pr, n in peers:
            copies.append(
                (
                    pltpu.make_async_remote_copy(
                        src_ref=src.at[n],
                        dst_ref=dst.at[me],
                        send_sem=ssem.at[n],
                        recv_sem=rsem.at[me],
                        device_id={"expert": pe, "dp": pr},
                        device_id_type=MESH,
                    ),
                    pltpu.make_async_remote_copy(
                        src_ref=src.at[n],
                        dst_ref=dst.at[n],
                        send_sem=ssem.at[n],
                        recv_sem=rsem.at[n],
                        device_id={"expert": pe, "dp": pr},
                        device_id_type=MESH,
                    ),
                )
            )
        return copies

    def slab(block):
        return jnp.concatenate([block[:, :half], block[:, half:]], 0).astype(BF16)

    def fill(dst, value):
        for pr in range(replicas):
            for pe in range(experts):
                dst[pr * experts + pe] = slab(
                    value[pe * CAP : (pe + 1) * CAP, pr * width : (pr + 1) * width]
                )

    tok_count = tokens.shape[0]
    top = expert_ids.shape[0]
    line = lax.broadcasted_iota(jnp.int32, (rows, tok_count), 0)
    owner = jnp.zeros((rows, tok_count), jnp.int32)
    for j in range(1, experts):
        owner = owner + (line >= j * CAP).astype(jnp.int32)
    place = (line - owner * CAP).astype(F32)
    token_down = lax.broadcasted_iota(jnp.int32, (tok_count, tok_count), 0)
    token_along = lax.broadcasted_iota(jnp.int32, (tok_count, tok_count), 1)
    earlier = (token_down < token_along).astype(F32).astype(BF16)
    loads[0].wait()
    picks = [(expert_ids[k : k + 1, :] == owner).astype(F32) for k in range(top)]
    named = functools.reduce(jnp.add, picks)
    here = jnp.where(dot(named.astype(BF16), earlier) == place, 1.0, 0.0)
    picks = [pick * here for pick in picks]
    either = (named * here).astype(BF16)
    loads[1].wait()
    fill(tok_send, dot(either, tokens[...]))
    pl.semaphore_wait(barrier, len(peers))

    tok_copies = exchange(tok_send, tok_recv, tok_ssem, tok_rsem)
    for out, _ in tok_copies:
        out.start()
    tok_recv[pl.ds(me, 1)] = tok_send[pl.ds(me, 1)]
    loads[2].wait()
    loads[3].wait()
    slot_weight = jnp.zeros((rows, 1), F32)
    weights = []
    for k in range(top):
        row = combine[k : k + 1, :]
        slot_weight = slot_weight + jnp.sum(picks[k] * row, 1, keepdims=True)
        weights.append(jnp.sum(jnp.where(token_down == token_along, row, 0.0), 1, keepdims=True))
    fill(grad_send, slot_weight * dot(either, out_grad[...]))
    picks = [pick.astype(BF16) for pick in picks]
    grad_recv[pl.ds(me, 1)] = grad_send[pl.ds(me, 1)]
    for load in loads[4:6]:
        load.wait()
    grad_copies = exchange(grad_send, grad_recv, grad_ssem, grad_rsem)

    def mate_copy(c, i):
        return pltpu.make_async_remote_copy(
            src_ref=mate_send.at[c, i],
            dst_ref=mate_recv.at[c, i],
            send_sem=mate_ssem.at[c, i],
            recv_sem=mate_rsem.at[c, i],
            device_id=mate,
            device_id_type=MESH,
        )

    def cross_copy(d, i):
        return pltpu.make_async_remote_copy(
            src_ref=cross_send.at[d, i],
            dst_ref=cross_recv.at[d, i],
            send_sem=cross_ssem.at[d, i],
            recv_sem=cross_rsem.at[d, i],
            device_id={"dp": lax.rem(chip + d, chips) * 2 + core},
            device_id_type=MESH,
        )

    for d in list(range(1, chips)) + [0]:
        for i in chip_peers[d]:
            tok_copies[i][1].wait_recv()
        if d == 0:
            for i in chip_peers[0]:
                grad_copies[i][0].start()
            for q in range(1, chips):
                for i in chip_peers[q]:
                    grad_copies[i][0].start()
        at = pl.ds(lax.rem(chip + d, chips) * 2 * experts, 2 * experts)
        x = tok_recv[at]
        lo, hi = x[:, :CAP].reshape(2 * rows, half), x[:, CAP:].reshape(2 * rows, half)
        for i, w in enumerate((gate_w, up_w)):
            part = dot(lo, w[:half]) + dot(hi, w[half:])
            for j in range(2):
                share = part[j * rows : (j + 1) * rows]

                @pl.when(core == j)
                def _():
                    own_sum[d, i] = share

                @pl.when(core != j)
                def _():
                    mate_send[d, i] = share.astype(BF16)

            mate_copy(d, i).start()

        for i in range(2):
            mate_copy(d, i).wait_recv()
            if d:
                cross_send[d, i] = (own_sum[d, i] + mate_recv[d, i].astype(F32)).astype(BF16)
                cross_copy(d, i).start()
            else:
                own_sum[0, i] = own_sum[0, i] + mate_recv[0, i].astype(F32)
    for d in range(1, chips):
        for i in range(2):
            cross_copy(d, i).wait_recv()
    total = own_sum[0]
    for d in range(1, chips):
        total = total + cross_recv[d].astype(F32)
    gate, up = total[0], total[1]
    hid[pl.ds(r, 1)] = ((gate / (1.0 + jnp.exp(-gate))) * up).astype(BF16)[None]

    def hid_copy(d, src, at, target, ssem, rsem):
        return pltpu.make_async_remote_copy(
            src_ref=hid.at[src],
            dst_ref=hid.at[at],
            send_sem=ssem.at[d],
            recv_sem=rsem.at[d],
            device_id={"dp": target},
            device_id_type=MESH,
        )

    hid_out, hid_in = [], []
    for d in range(1, chips):
        ahead = lax.rem(chip + d, chips) * 2 + core
        behind = lax.rem(chip + chips - d, chips) * 2 + core
        hid_out.append(hid_copy(d, r, r, ahead, hid_ssem, hid_rsem))
        hid_in.append(hid_copy(d, r, behind, ahead, hid_ssem, hid_rsem))
    for copy in hid_out:
        copy.start()
    mate_r = chip * 2 + 1 - core
    mate_out = hid_copy(0, r, r, mate_r, fwd_ssem, fwd_rsem)
    mate_in = hid_copy(0, r, mate_r, mate_r, fwd_ssem, fwd_rsem)
    mate_out.start()
    loads[6].wait()

    ret_copies = exchange(ret_send, ret_recv, ret_ssem, ret_rsem)

    def give_back(pr):
        out = dot(hid[pr], down_w[...], ((1,), (1,)))
        for pe in range(experts):
            ret_send[pr * experts + pe] = slab(out[pe * CAP : (pe + 1) * CAP])

    def send_back(dr_pr, skip_self):
        for de in range(experts):
            if skip_self and de == 0:
                continue
            pe = lax.rem(e + de, experts)
            n = dr_pr * experts + pe
            pltpu.make_async_remote_copy(
                src_ref=ret_send.at[n],
                dst_ref=ret_recv.at[me],
                send_sem=ret_ssem.at[n],
                recv_sem=ret_rsem.at[me],
                device_id={"expert": pe, "dp": dr_pr},
                device_id_type=MESH,
            ).start()

    give_back(r)
    send_back(r, True)
    ret_recv[pl.ds(me, 1)] = ret_send[pl.ds(me, 1)]
    mate_in.wait_recv()
    give_back(mate_r)
    send_back(mate_r, False)
    forwards = []
    for d in range(1, chips):
        hid_in[d - 1].wait_recv()
        behind = lax.rem(chip + chips - d, chips)
        out = hid_copy(d, behind * 2 + core, behind * 2 + core, mate_r, fwd_ssem, fwd_rsem)
        into = hid_copy(d, behind * 2 + core, behind * 2 + 1 - core, mate_r, fwd_ssem, fwd_rsem)
        out.start()
        forwards.append((out, into))
        give_back(behind * 2 + core)
        send_back(behind * 2 + core, False)
    for d in range(1, chips):
        forwards[d - 1][1].wait_recv()
        behind = lax.rem(chip + chips - d, chips)
        give_back(behind * 2 + 1 - core)
        send_back(behind * 2 + 1 - core, False)

    for _, back in grad_copies:
        back.wait_recv()
    hidden = hid[...].reshape(replicas * rows, ff)
    for h in range(2):
        g = grad_recv[:, h * CAP : (h + 1) * CAP].reshape(replicas * rows, half)
        down_grad[h * half : (h + 1) * half] = dot(g, hidden, ((0,), (0,))).astype(BF16)

    store_grad = pltpu.make_async_copy(down_grad, down_grad_hbm, store_sem.at[0])
    store_grad.start()
    arrivals = [r, mate_r]
    for d in range(1, chips):
        arrivals.append(lax.rem(chip + chips - d, chips) * 2 + core)
    for d in range(1, chips):
        arrivals.append(lax.rem(chip + chips - d, chips) * 2 + 1 - core)
    for number, pr in enumerate(arrivals):
        for de in range(1 if number == 0 else 0, experts):
            n = pr * experts + lax.rem(e + de, experts)
            pltpu.make_async_remote_copy(
                src_ref=ret_send.at[n],
                dst_ref=ret_recv.at[n],
                send_sem=ret_ssem.at[n],
                recv_sem=ret_rsem.at[n],
                device_id={"expert": lax.rem(e + de, experts), "dp": pr},
                device_id_type=MESH,
            ).wait_recv()
        arrived = ret_recv[pl.ds(pr * experts, experts)]
        for h in range(2):
            block = arrived[:, h * CAP : (h + 1) * CAP]
            block = block.reshape(rows, half)
            value = weights[0] * dot(picks[0], block, ((0,), (0,)))
            for k in range(1, top):
                value = value + weights[k] * dot(picks[k], block, ((0,), (0,)))
            start = pl.multiple_of(pr * width + h * half, 128)
            mixed[:, pl.ds(start, half)] = value.astype(BF16)

    store_mixed = pltpu.make_async_copy(mixed, mixed_hbm, store_sem.at[1])
    store_mixed.start()
    for copies in (tok_copies, grad_copies, ret_copies):
        for out, _ in copies:
            out.wait_send()
    for i in range(2):
        for d in range(chips):
            mate_copy(d, i).wait_send()
        for d in range(1, chips):
            cross_copy(d, i).wait_send()
    for copy in hid_out:
        copy.wait_send()
    mate_out.wait_send()
    for out, _ in forwards:
        out.wait_send()
    store_grad.wait()
    store_mixed.wait()


def tokens_move(tokens, out_grad, expert_ids, combine, gate_weight, up_weight, down_t):
    experts, replicas = lax.axis_size("expert"), lax.axis_size("dp")
    _, width, ff = gate_weight.shape
    top = expert_ids.shape[1]
    peers, chips, rows = experts * replicas, replicas // 2, experts * CAP
    slabs = pltpu.VMEM((peers, 2 * CAP, width // 2), BF16)
    dma = pltpu.SemaphoreType.DMA
    hbm = pl.BlockSpec(memory_space=pl.ANY)
    mixed, down_grad = pl.pallas_call(
        functools.partial(kernel, experts, replicas),
        out_shape=(
            jax.ShapeDtypeStruct(tokens.shape, BF16),
            jax.ShapeDtypeStruct((width, ff), BF16),
        ),
        in_specs=[hbm] * 7,
        out_specs=(hbm, hbm),
        scratch_shapes=[pltpu.VMEM((width, ff), BF16)] * 3
        + [pltpu.VMEM(tokens.shape, BF16)] * 2
        + [pltpu.VMEM((top, tokens.shape[0]), jnp.int32)]
        + [pltpu.VMEM((top, tokens.shape[0]), F32)]
        + [pltpu.VMEM(tokens.shape, BF16), pltpu.VMEM((width, ff), BF16)]
        + [slabs] * 6
        + [pltpu.VMEM((chips, 2, rows, ff), BF16)] * 4
        + [pltpu.VMEM((chips, 2, rows, ff), F32), pltpu.VMEM((replicas, rows, ff), BF16)]
        + [dma((7,)), dma((2,))]
        + [dma((peers,))] * 6
        + [dma((chips, 2))] * 4
        + [dma((chips,))] * 4,
        compiler_params=pltpu.CompilerParams(
            collective_id=0, has_side_effects=True, vmem_limit_bytes=60 * 1024 * 1024
        ),
    )(tokens, out_grad, expert_ids.T, combine.T, gate_weight[0], up_weight[0], down_t[0])
    return mixed, down_grad[None]


def weights_move(tokens, out_grad, expert_ids, combine, gate_weight, up_weight, down_t):
    experts = lax.axis_size("expert")
    tok_count, top_count = expert_ids.shape
    model_width = tokens.shape[1]
    slot_total = experts * CAP
    flat_ids = expert_ids.reshape(-1)
    onehot = (flat_ids[:, None] == jnp.arange(experts, dtype=jnp.int32)[None, :]).astype(jnp.int32)
    earlier = jnp.sum((jnp.cumsum(onehot, 0) - onehot) * onehot, 1)
    target = flat_ids * CAP + earlier
    sources = jnp.arange(tok_count * top_count, dtype=jnp.int32) // top_count
    slot_token = jnp.full((slot_total,), tok_count, jnp.int32).at[target].set(sources)
    slot_weight = jnp.zeros((slot_total,), jnp.float32).at[target].set(combine.reshape(-1))
    padded_rows = jnp.concatenate([tokens, jnp.zeros((1, model_width), jnp.bfloat16)], 0)
    padded_grad = jnp.concatenate([out_grad, jnp.zeros((1, model_width), jnp.bfloat16)], 0)
    send_rows = padded_rows[slot_token].reshape(experts, CAP, model_width)
    send_grad = (slot_weight[:, None] * padded_grad[slot_token].astype(jnp.float32)).astype(
        jnp.bfloat16
    )
    send_grad = send_grad.reshape(experts, CAP, model_width)
    recv_rows = lax.all_to_all(send_rows, "expert", split_axis=0, concat_axis=0, tiled=True)
    expert_rows = recv_rows.reshape(slot_total, model_width)
    gate_shard = gate_weight[0]
    up_shard = up_weight[0]
    down_shard = down_t[0]

    def add_rows(shard_piece):
        return jnp.dot(expert_rows, shard_piece, preferred_element_type=jnp.float32)

    gate_sum = add_rows(lax.all_gather(gate_shard, "dp", axis=0, tiled=True))
    up_sum = add_rows(lax.all_gather(up_shard, "dp", axis=0, tiled=True))
    hidden = (jax.nn.silu(gate_sum) * up_sum).astype(jnp.bfloat16)
    product = lax.dot_general(
        hidden,
        lax.all_gather(down_shard, "dp", axis=0, tiled=True),
        (((1,), (1,)), ((), ())),
        preferred_element_type=jnp.float32,
    )
    expert_out = product.astype(jnp.bfloat16)
    returned = lax.all_to_all(
        expert_out.reshape(experts, CAP, model_width),
        "expert",
        split_axis=0,
        concat_axis=0,
        tiled=True,
    )
    returned = returned.reshape(slot_total, model_width)[target]
    mixed = jnp.sum(
        returned.reshape(tok_count, top_count, model_width).astype(jnp.float32)
        * combine[:, :, None],
        1,
    )
    mixed = mixed.astype(jnp.bfloat16)
    recv_grad = lax.all_to_all(send_grad, "expert", split_axis=0, concat_axis=0, tiled=True)
    grad_rows = recv_grad.reshape(slot_total, model_width)
    own_grad = lax.psum_scatter(
        lax.dot_general(
            grad_rows, hidden, (((0,), (0,)), ((), ())), preferred_element_type=jnp.float32
        ).astype(jnp.bfloat16),
        "dp",
        scatter_dimension=0,
        tiled=True,
    )
    down_grad = own_grad[None]
    return (mixed, down_grad)


def solution(mesh):
    in_specs = (
        P(("group", "expert", "dp"), None),
        P(("group", "expert", "dp"), None),
        P(("group", "expert", "dp"), None),
        P(("group", "expert", "dp"), None),
        P("expert", "dp", None),
        P("expert", "dp", None),
        P("expert", "dp", None),
    )
    out_specs = (P(("group", "expert", "dp"), None), P(("group", "expert"), "dp", None))

    def per_device(*args):
        experts, replicas = lax.axis_size("expert"), lax.axis_size("dp")
        features, ff = args[0].shape[1], args[4].shape[2]
        slots = experts * replicas * CAP
        moved_tokens = slots * (3 * features // replicas + 3 * ff)
        moved_weights = 4 * features * ff + 3 * experts * CAP * features
        small = moved_tokens < moved_weights and slots <= 1024
        if small and replicas % 2 == 0 and features % (256 * replicas) == 0:
            return tokens_move(*args)
        return weights_move(*args)

    return jax.shard_map(
        per_device, mesh=mesh, in_specs=in_specs, out_specs=out_specs, check_vma=False
    )
```

```python
import functools

import jax
import jax.numpy as jnp
from jax import lax
from jax.experimental import pallas as pl
from jax.experimental.pallas import tpu as pltpu
from jax.sharding import PartitionSpec as P

CAP = 24
MESH = pl.DeviceIdType.MESH
F32 = jnp.float32
BF16 = jnp.bfloat16


def dot(a, b, dims=((1,), (0,))):
    return lax.dot_general(a, b, (dims, ((), ())), preferred_element_type=F32)


def kernel(
    experts,
    replicas,
    tokens_hbm,
    out_grad_hbm,
    ids_hbm,
    combine_hbm,
    gate_hbm,
    up_hbm,
    down_hbm,
    mixed,
    down_grad,
    gate_w,
    up_w,
    down_w,
    tokens,
    out_grad,
    expert_ids,
    combine,
    tok_send,
    tok_recv,
    grad_send,
    grad_recv,
    ret_send,
    ret_recv,
    mate_send,
    mate_recv,
    cross_send,
    cross_recv,
    own_sum,
    hid,
    load_sem,
    tok_ssem,
    tok_rsem,
    grad_ssem,
    grad_rsem,
    ret_ssem,
    ret_rsem,
    mate_ssem,
    mate_rsem,
    cross_ssem,
    cross_rsem,
    hid_ssem,
    hid_rsem,
    fwd_ssem,
    fwd_rsem,
):
    width = gate_hbm.shape[0]
    half = width // 2
    ff = gate_hbm.shape[1]
    rows = experts * CAP
    chips = replicas // 2
    e = lax.axis_index("expert")
    r = lax.axis_index("dp")
    chip = r // 2
    core = r % 2
    me = r * experts + e
    mate = {"dp": chip * 2 + 1 - core}

    loads = [
        pltpu.make_async_copy(src, dst, load_sem.at[i])
        for i, (src, dst) in enumerate(
            (
                (ids_hbm, expert_ids),
                (tokens_hbm, tokens),
                (combine_hbm, combine),
                (out_grad_hbm, out_grad),
                (gate_hbm, gate_w),
                (up_hbm, up_w),
                (down_hbm, down_w),
            )
        )
    ]
    for load in loads[:4]:
        load.start()

    peers, chip_peers = [], {}
    for d in list(range(1, chips)) + [0]:
        chip_peers[d] = []
        for dc in range(2):
            for de in range(experts):
                if d or dc or de:
                    pe = lax.rem(e + de, experts)
                    pr = lax.rem(chip + d, chips) * 2 + lax.rem(core + dc, 2)
                    chip_peers[d].append(len(peers))
                    peers.append((pe, pr, pr * experts + pe))
    barrier = pltpu.get_barrier_semaphore()
    for pe, pr, _ in peers:
        pl.semaphore_signal(barrier, inc=1, device_id={"expert": pe, "dp": pr}, device_id_type=MESH)

    for load in loads[4:]:
        load.start()

    def exchange(src, dst, ssem, rsem):
        copies = []
        for pe, pr, n in peers:
            copies.append(
                (
                    pltpu.make_async_remote_copy(
                        src_ref=src.at[n],
                        dst_ref=dst.at[me],
                        send_sem=ssem.at[n],
                        recv_sem=rsem.at[me],
                        device_id={"expert": pe, "dp": pr},
                        device_id_type=MESH,
                    ),
                    pltpu.make_async_remote_copy(
                        src_ref=src.at[n],
                        dst_ref=dst.at[n],
                        send_sem=ssem.at[n],
                        recv_sem=rsem.at[n],
                        device_id={"expert": pe, "dp": pr},
                        device_id_type=MESH,
                    ),
                )
            )
        return copies

    def slab(block):
        return jnp.concatenate([block[:, :half], block[:, half:]], 0).astype(BF16)

    def fill(dst, value):
        for pr in range(replicas):
            for pe in range(experts):
                dst[pr * experts + pe] = slab(
                    value[pe * CAP : (pe + 1) * CAP, pr * width : (pr + 1) * width]
                )

    tok_count = tokens.shape[0]
    top = expert_ids.shape[0]
    line = lax.broadcasted_iota(jnp.int32, (rows, tok_count), 0)
    owner = jnp.zeros((rows, tok_count), jnp.int32)
    for j in range(1, experts):
        owner = owner + (line >= j * CAP).astype(jnp.int32)
    place = (line - owner * CAP).astype(F32)
    token_down = lax.broadcasted_iota(jnp.int32, (tok_count, tok_count), 0)
    token_along = lax.broadcasted_iota(jnp.int32, (tok_count, tok_count), 1)
    earlier = (token_down < token_along).astype(F32).astype(BF16)
    loads[0].wait()
    picks = [(expert_ids[k : k + 1, :] == owner).astype(F32) for k in range(top)]
    named = functools.reduce(jnp.add, picks)
    here = jnp.where(dot(named.astype(BF16), earlier) == place, 1.0, 0.0)
    picks = [pick * here for pick in picks]
    either = (named * here).astype(BF16)
    loads[1].wait()
    fill(tok_send, dot(either, tokens[...]))
    pl.semaphore_wait(barrier, len(peers))

    tok_copies = exchange(tok_send, tok_recv, tok_ssem, tok_rsem)
    for out, _ in tok_copies:
        out.start()
    tok_recv[pl.ds(me, 1)] = tok_send[pl.ds(me, 1)]
    loads[2].wait()
    loads[3].wait()
    slot_weight = jnp.zeros((rows, 1), F32)
    weights = []
    for k in range(top):
        row = combine[k : k + 1, :]
        slot_weight = slot_weight + jnp.sum(picks[k] * row, 1, keepdims=True)
        weights.append(jnp.sum(jnp.where(token_down == token_along, row, 0.0), 1, keepdims=True))
    fill(grad_send, slot_weight * dot(either, out_grad[...]))
    picks = [pick.astype(BF16) for pick in picks]
    grad_recv[pl.ds(me, 1)] = grad_send[pl.ds(me, 1)]
    for load in loads[4:6]:
        load.wait()
    grad_copies = exchange(grad_send, grad_recv, grad_ssem, grad_rsem)

    def mate_copy(c, i):
        return pltpu.make_async_remote_copy(
            src_ref=mate_send.at[c, i],
            dst_ref=mate_recv.at[c, i],
            send_sem=mate_ssem.at[c, i],
            recv_sem=mate_rsem.at[c, i],
            device_id=mate,
            device_id_type=MESH,
        )

    def cross_copy(d, i):
        return pltpu.make_async_remote_copy(
            src_ref=cross_send.at[d, i],
            dst_ref=cross_recv.at[d, i],
            send_sem=cross_ssem.at[d, i],
            recv_sem=cross_rsem.at[d, i],
            device_id={"dp": lax.rem(chip + d, chips) * 2 + core},
            device_id_type=MESH,
        )

    for d in list(range(1, chips)) + [0]:
        for i in chip_peers[d]:
            tok_copies[i][1].wait_recv()
        if d == 0:
            for i in chip_peers[0]:
                grad_copies[i][0].start()
            for q in range(1, chips):
                for i in chip_peers[q]:
                    grad_copies[i][0].start()
        at = pl.ds(lax.rem(chip + d, chips) * 2 * experts, 2 * experts)
        x = tok_recv[at]
        lo, hi = x[:, :CAP].reshape(2 * rows, half), x[:, CAP:].reshape(2 * rows, half)
        for i, w in enumerate((gate_w, up_w)):
            part = dot(lo, w[:half]) + dot(hi, w[half:])
            for j in range(2):
                share = part[j * rows : (j + 1) * rows]

                @pl.when(core == j)
                def _():
                    own_sum[d, i] = share

                @pl.when(core != j)
                def _():
                    mate_send[d, i] = share.astype(BF16)

            mate_copy(d, i).start()

        for i in range(2):
            mate_copy(d, i).wait_recv()
            if d:
                cross_send[d, i] = (own_sum[d, i] + mate_recv[d, i].astype(F32)).astype(BF16)
                cross_copy(d, i).start()
            else:
                own_sum[0, i] = own_sum[0, i] + mate_recv[0, i].astype(F32)
    for d in range(1, chips):
        for i in range(2):
            cross_copy(d, i).wait_recv()
    total = own_sum[0]
    for d in range(1, chips):
        total = total + cross_recv[d].astype(F32)
    gate, up = total[0], total[1]
    hid[pl.ds(r, 1)] = ((gate / (1.0 + jnp.exp(-gate))) * up).astype(BF16)[None]

    def hid_copy(d, src, at, target, ssem, rsem):
        return pltpu.make_async_remote_copy(
            src_ref=hid.at[src],
            dst_ref=hid.at[at],
            send_sem=ssem.at[d],
            recv_sem=rsem.at[d],
            device_id={"dp": target},
            device_id_type=MESH,
        )

    hid_out, hid_in = [], []
    for d in range(1, chips):
        ahead = lax.rem(chip + d, chips) * 2 + core
        behind = lax.rem(chip + chips - d, chips) * 2 + core
        hid_out.append(hid_copy(d, r, r, ahead, hid_ssem, hid_rsem))
        hid_in.append(hid_copy(d, r, behind, ahead, hid_ssem, hid_rsem))
    for copy in hid_out:
        copy.start()
    mate_r = chip * 2 + 1 - core
    mate_out = hid_copy(0, r, r, mate_r, fwd_ssem, fwd_rsem)
    mate_in = hid_copy(0, r, mate_r, mate_r, fwd_ssem, fwd_rsem)
    mate_out.start()
    loads[6].wait()

    ret_copies = exchange(ret_send, ret_recv, ret_ssem, ret_rsem)

    def give_back(pr):
        out = dot(hid[pr], down_w[...], ((1,), (1,)))
        for pe in range(experts):
            ret_send[pr * experts + pe] = slab(out[pe * CAP : (pe + 1) * CAP])

    def send_back(dr_pr, skip_self):
        for de in range(experts):
            if skip_self and de == 0:
                continue
            pe = lax.rem(e + de, experts)
            n = dr_pr * experts + pe
            pltpu.make_async_remote_copy(
                src_ref=ret_send.at[n],
                dst_ref=ret_recv.at[me],
                send_sem=ret_ssem.at[n],
                recv_sem=ret_rsem.at[me],
                device_id={"expert": pe, "dp": dr_pr},
                device_id_type=MESH,
            ).start()

    give_back(r)
    send_back(r, True)
    ret_recv[pl.ds(me, 1)] = ret_send[pl.ds(me, 1)]
    mate_in.wait_recv()
    give_back(mate_r)
    send_back(mate_r, False)
    forwards = []
    for d in range(1, chips):
        hid_in[d - 1].wait_recv()
        behind = lax.rem(chip + chips - d, chips)
        out = hid_copy(d, behind * 2 + core, behind * 2 + core, mate_r, fwd_ssem, fwd_rsem)
        into = hid_copy(d, behind * 2 + core, behind * 2 + 1 - core, mate_r, fwd_ssem, fwd_rsem)
        out.start()
        forwards.append((out, into))
        give_back(behind * 2 + core)
        send_back(behind * 2 + core, False)
    for d in range(1, chips):
        forwards[d - 1][1].wait_recv()
        behind = lax.rem(chip + chips - d, chips)
        give_back(behind * 2 + 1 - core)
        send_back(behind * 2 + 1 - core, False)

    for _, back in grad_copies:
        back.wait_recv()
    hidden = hid[...].reshape(replicas * rows, ff)
    for h in range(2):
        g = grad_recv[:, h * CAP : (h + 1) * CAP].reshape(replicas * rows, half)
        down_grad[h * half : (h + 1) * half] = dot(g, hidden, ((0,), (0,))).astype(BF16)

    arrivals = [r, mate_r]
    for d in range(1, chips):
        arrivals.append(lax.rem(chip + chips - d, chips) * 2 + core)
    for d in range(1, chips):
        arrivals.append(lax.rem(chip + chips - d, chips) * 2 + 1 - core)
    for number, pr in enumerate(arrivals):
        for de in range(1 if number == 0 else 0, experts):
            n = pr * experts + lax.rem(e + de, experts)
            pltpu.make_async_remote_copy(
                src_ref=ret_send.at[n],
                dst_ref=ret_recv.at[n],
                send_sem=ret_ssem.at[n],
                recv_sem=ret_rsem.at[n],
                device_id={"expert": lax.rem(e + de, experts), "dp": pr},
                device_id_type=MESH,
            ).wait_recv()
        arrived = ret_recv[pl.ds(pr * experts, experts)]
        for h in range(2):
            block = arrived[:, h * CAP : (h + 1) * CAP]
            block = block.reshape(rows, half)
            value = weights[0] * dot(picks[0], block, ((0,), (0,)))
            for k in range(1, top):
                value = value + weights[k] * dot(picks[k], block, ((0,), (0,)))
            start = pl.multiple_of(pr * width + h * half, 128)
            mixed[:, pl.ds(start, half)] = value.astype(BF16)

    for copies in (tok_copies, grad_copies, ret_copies):
        for out, _ in copies:
            out.wait_send()
    for i in range(2):
        for d in range(chips):
            mate_copy(d, i).wait_send()
        for d in range(1, chips):
            cross_copy(d, i).wait_send()
    for copy in hid_out:
        copy.wait_send()
    mate_out.wait_send()
    for out, _ in forwards:
        out.wait_send()


def tokens_move(tokens, out_grad, expert_ids, combine, gate_weight, up_weight, down_t):
    experts, replicas = lax.axis_size("expert"), lax.axis_size("dp")
    _, width, ff = gate_weight.shape
    top = expert_ids.shape[1]
    peers, chips, rows = experts * replicas, replicas // 2, experts * CAP
    slabs = pltpu.VMEM((peers, 2 * CAP, width // 2), BF16)
    dma = pltpu.SemaphoreType.DMA
    hbm = pl.BlockSpec(memory_space=pl.ANY)
    mixed, down_grad = pl.pallas_call(
        functools.partial(kernel, experts, replicas),
        out_shape=(
            pltpu.VMEM(tokens.shape, BF16),
            pltpu.VMEM((width, ff), BF16),
        ),
        in_specs=[hbm] * 7,
        out_specs=(pl.BlockSpec(memory_space=pltpu.VMEM),) * 2,
        scratch_shapes=[pltpu.VMEM((width, ff), BF16)] * 3
        + [pltpu.VMEM(tokens.shape, BF16)] * 2
        + [pltpu.VMEM((top, tokens.shape[0]), jnp.int32)]
        + [pltpu.VMEM((top, tokens.shape[0]), F32)]
        + [slabs] * 6
        + [pltpu.VMEM((chips, 2, rows, ff), BF16)] * 4
        + [pltpu.VMEM((chips, 2, rows, ff), F32), pltpu.VMEM((replicas, rows, ff), BF16)]
        + [dma((7,))]
        + [dma((peers,))] * 6
        + [dma((chips, 2))] * 4
        + [dma((chips,))] * 4,
        compiler_params=pltpu.CompilerParams(
            collective_id=0, has_side_effects=True, vmem_limit_bytes=60 * 1024 * 1024
        ),
    )(tokens, out_grad, expert_ids.T, combine.T, gate_weight[0], up_weight[0], down_t[0])
    return mixed, down_grad[None]


def weights_move(tokens, out_grad, expert_ids, combine, gate_weight, up_weight, down_t):
    experts = lax.axis_size("expert")
    tok_count, top_count = expert_ids.shape
    model_width = tokens.shape[1]
    slot_total = experts * CAP
    flat_ids = expert_ids.reshape(-1)
    onehot = (flat_ids[:, None] == jnp.arange(experts, dtype=jnp.int32)[None, :]).astype(jnp.int32)
    earlier = jnp.sum((jnp.cumsum(onehot, 0) - onehot) * onehot, 1)
    target = flat_ids * CAP + earlier
    sources = jnp.arange(tok_count * top_count, dtype=jnp.int32) // top_count
    slot_token = jnp.full((slot_total,), tok_count, jnp.int32).at[target].set(sources)
    slot_weight = jnp.zeros((slot_total,), jnp.float32).at[target].set(combine.reshape(-1))
    padded_rows = jnp.concatenate([tokens, jnp.zeros((1, model_width), jnp.bfloat16)], 0)
    padded_grad = jnp.concatenate([out_grad, jnp.zeros((1, model_width), jnp.bfloat16)], 0)
    send_rows = padded_rows[slot_token].reshape(experts, CAP, model_width)
    send_grad = (slot_weight[:, None] * padded_grad[slot_token].astype(jnp.float32)).astype(
        jnp.bfloat16
    )
    send_grad = send_grad.reshape(experts, CAP, model_width)
    recv_rows = lax.all_to_all(send_rows, "expert", split_axis=0, concat_axis=0, tiled=True)
    expert_rows = recv_rows.reshape(slot_total, model_width)
    gate_shard = gate_weight[0]
    up_shard = up_weight[0]
    down_shard = down_t[0]

    def add_rows(shard_piece):
        return jnp.dot(expert_rows, shard_piece, preferred_element_type=jnp.float32)

    gate_sum = add_rows(lax.all_gather(gate_shard, "dp", axis=0, tiled=True))
    up_sum = add_rows(lax.all_gather(up_shard, "dp", axis=0, tiled=True))
    hidden = (jax.nn.silu(gate_sum) * up_sum).astype(jnp.bfloat16)
    product = lax.dot_general(
        hidden,
        lax.all_gather(down_shard, "dp", axis=0, tiled=True),
        (((1,), (1,)), ((), ())),
        preferred_element_type=jnp.float32,
    )
    expert_out = product.astype(jnp.bfloat16)
    returned = lax.all_to_all(
        expert_out.reshape(experts, CAP, model_width),
        "expert",
        split_axis=0,
        concat_axis=0,
        tiled=True,
    )
    returned = returned.reshape(slot_total, model_width)[target]
    mixed = jnp.sum(
        returned.reshape(tok_count, top_count, model_width).astype(jnp.float32)
        * combine[:, :, None],
        1,
    )
    mixed = mixed.astype(jnp.bfloat16)
    recv_grad = lax.all_to_all(send_grad, "expert", split_axis=0, concat_axis=0, tiled=True)
    grad_rows = recv_grad.reshape(slot_total, model_width)
    own_grad = lax.psum_scatter(
        lax.dot_general(
            grad_rows, hidden, (((0,), (0,)), ((), ())), preferred_element_type=jnp.float32
        ).astype(jnp.bfloat16),
        "dp",
        scatter_dimension=0,
        tiled=True,
    )
    down_grad = own_grad[None]
    return (mixed, down_grad)


def solution(mesh):
    in_specs = (
        P(("group", "expert", "dp"), None),
        P(("group", "expert", "dp"), None),
        P(("group", "expert", "dp"), None),
        P(("group", "expert", "dp"), None),
        P("expert", "dp", None),
        P("expert", "dp", None),
        P("expert", "dp", None),
    )
    out_specs = (P(("group", "expert", "dp"), None), P(("group", "expert"), "dp", None))

    def per_device(*args):
        experts, replicas = lax.axis_size("expert"), lax.axis_size("dp")
        features, ff = args[0].shape[1], args[4].shape[2]
        slots = experts * replicas * CAP
        moved_tokens = slots * (3 * features // replicas + 3 * ff)
        moved_weights = 4 * features * ff + 3 * experts * CAP * features
        small = moved_tokens < moved_weights and slots <= 1024
        if small and replicas % 2 == 0 and features % (256 * replicas) == 0:
            return tokens_move(*args)
        return weights_move(*args)

    return jax.shard_map(
        per_device, mesh=mesh, in_specs=in_specs, out_specs=out_specs, check_vma=False
    )
```

```python
import functools

import jax
import jax.numpy as jnp
from jax import lax
from jax.experimental import pallas as pl
from jax.experimental.pallas import tpu as pltpu
from jax.sharding import PartitionSpec as P

CAP = 24
MESH = pl.DeviceIdType.MESH
F32 = jnp.float32
BF16 = jnp.bfloat16


def dot(a, b, dims=((1,), (0,))):
    return lax.dot_general(a, b, (dims, ((), ())), preferred_element_type=F32)


def kernel(
    experts,
    replicas,
    tokens_hbm,
    out_grad_hbm,
    ids_hbm,
    combine_hbm,
    gate_hbm,
    up_hbm,
    down_hbm,
    mixed,
    down_grad,
    gate_w,
    up_w,
    down_w,
    tokens,
    out_grad,
    expert_ids,
    combine,
    down_t,
    tok_send,
    tok_recv,
    grad_send,
    grad_recv,
    ret_send,
    ret_recv,
    mate_send,
    mate_recv,
    cross_send,
    cross_recv,
    own_sum,
    hid,
    load_sem,
    tok_ssem,
    tok_rsem,
    grad_ssem,
    grad_rsem,
    ret_ssem,
    ret_rsem,
    mate_ssem,
    mate_rsem,
    cross_ssem,
    cross_rsem,
    hid_ssem,
    hid_rsem,
    fwd_ssem,
    fwd_rsem,
):
    width = gate_hbm.shape[0]
    half = width // 2
    ff = gate_hbm.shape[1]
    rows = experts * CAP
    chips = replicas // 2
    e = lax.axis_index("expert")
    r = lax.axis_index("dp")
    chip = r // 2
    core = r % 2
    me = r * experts + e
    mate = {"dp": chip * 2 + 1 - core}

    loads = [
        pltpu.make_async_copy(src, dst, load_sem.at[i])
        for i, (src, dst) in enumerate(
            (
                (ids_hbm, expert_ids),
                (tokens_hbm, tokens),
                (combine_hbm, combine),
                (out_grad_hbm, out_grad),
                (gate_hbm, gate_w),
                (up_hbm, up_w),
                (down_hbm, down_w),
            )
        )
    ]
    for load in loads[:4]:
        load.start()

    peers, chip_peers = [], {}
    for d in list(range(1, chips)) + [0]:
        chip_peers[d] = []
        for dc in range(2):
            for de in range(experts):
                if d or dc or de:
                    pe = lax.rem(e + de, experts)
                    pr = lax.rem(chip + d, chips) * 2 + lax.rem(core + dc, 2)
                    chip_peers[d].append(len(peers))
                    peers.append((pe, pr, pr * experts + pe))
    barrier = pltpu.get_barrier_semaphore()
    for pe, pr, _ in peers:
        pl.semaphore_signal(barrier, inc=1, device_id={"expert": pe, "dp": pr}, device_id_type=MESH)

    for load in loads[4:]:
        load.start()

    def exchange(src, dst, ssem, rsem):
        copies = []
        for pe, pr, n in peers:
            copies.append(
                (
                    pltpu.make_async_remote_copy(
                        src_ref=src.at[n],
                        dst_ref=dst.at[me],
                        send_sem=ssem.at[n],
                        recv_sem=rsem.at[me],
                        device_id={"expert": pe, "dp": pr},
                        device_id_type=MESH,
                    ),
                    pltpu.make_async_remote_copy(
                        src_ref=src.at[n],
                        dst_ref=dst.at[n],
                        send_sem=ssem.at[n],
                        recv_sem=rsem.at[n],
                        device_id={"expert": pe, "dp": pr},
                        device_id_type=MESH,
                    ),
                )
            )
        return copies

    def slab(block):
        return jnp.concatenate([block[:, :half], block[:, half:]], 0).astype(BF16)

    def fill(dst, value):
        for pr in range(replicas):
            for pe in range(experts):
                dst[pr * experts + pe] = slab(
                    value[pe * CAP : (pe + 1) * CAP, pr * width : (pr + 1) * width]
                )

    tok_count = tokens.shape[0]
    top = expert_ids.shape[0]
    line = lax.broadcasted_iota(jnp.int32, (rows, tok_count), 0)
    owner = jnp.zeros((rows, tok_count), jnp.int32)
    for j in range(1, experts):
        owner = owner + (line >= j * CAP).astype(jnp.int32)
    place = (line - owner * CAP).astype(F32)
    token_down = lax.broadcasted_iota(jnp.int32, (tok_count, tok_count), 0)
    token_along = lax.broadcasted_iota(jnp.int32, (tok_count, tok_count), 1)
    earlier = (token_down < token_along).astype(F32).astype(BF16)
    loads[0].wait()
    picks = [(expert_ids[k : k + 1, :] == owner).astype(F32) for k in range(top)]
    named = functools.reduce(jnp.add, picks)
    here = jnp.where(dot(named.astype(BF16), earlier) == place, 1.0, 0.0)
    picks = [pick * here for pick in picks]
    either = (named * here).astype(BF16)
    loads[1].wait()
    fill(tok_send, dot(either, tokens[...]))
    pl.semaphore_wait(barrier, len(peers))

    tok_copies = exchange(tok_send, tok_recv, tok_ssem, tok_rsem)
    for out, _ in tok_copies:
        out.start()
    tok_recv[pl.ds(me, 1)] = tok_send[pl.ds(me, 1)]
    loads[2].wait()
    loads[3].wait()
    slot_weight = jnp.zeros((rows, 1), F32)
    weights = []
    for k in range(top):
        row = combine[k : k + 1, :]
        slot_weight = slot_weight + jnp.sum(picks[k] * row, 1, keepdims=True)
        weights.append(jnp.sum(jnp.where(token_down == token_along, row, 0.0), 1, keepdims=True))
    fill(grad_send, slot_weight * dot(either, out_grad[...]))
    picks = [pick.astype(BF16) for pick in picks]
    grad_recv[pl.ds(me, 1)] = grad_send[pl.ds(me, 1)]
    for load in loads[4:]:
        load.wait()
    down_t[...] = down_w[...].T
    grad_copies = exchange(grad_send, grad_recv, grad_ssem, grad_rsem)

    def mate_copy(c, i):
        return pltpu.make_async_remote_copy(
            src_ref=mate_send.at[c, i],
            dst_ref=mate_recv.at[c, i],
            send_sem=mate_ssem.at[c, i],
            recv_sem=mate_rsem.at[c, i],
            device_id=mate,
            device_id_type=MESH,
        )

    def cross_copy(d, i):
        return pltpu.make_async_remote_copy(
            src_ref=cross_send.at[d, i],
            dst_ref=cross_recv.at[d, i],
            send_sem=cross_ssem.at[d, i],
            recv_sem=cross_rsem.at[d, i],
            device_id={"dp": lax.rem(chip + d, chips) * 2 + core},
            device_id_type=MESH,
        )

    for d in list(range(1, chips)) + [0]:
        for i in chip_peers[d]:
            tok_copies[i][1].wait_recv()
        if d == 0:
            for i in chip_peers[0]:
                grad_copies[i][0].start()
            for q in range(1, chips):
                for i in chip_peers[q]:
                    grad_copies[i][0].start()
        at = pl.ds(lax.rem(chip + d, chips) * 2 * experts, 2 * experts)
        x = tok_recv[at]
        lo, hi = x[:, :CAP].reshape(2 * rows, half), x[:, CAP:].reshape(2 * rows, half)
        for i, w in enumerate((gate_w, up_w)):
            part = dot(lo, w[:half]) + dot(hi, w[half:])
            for j in range(2):
                share = part[j * rows : (j + 1) * rows]

                @pl.when(core == j)
                def _():
                    own_sum[d, i] = share

                @pl.when(core != j)
                def _():
                    mate_send[d, i] = share.astype(BF16)

            mate_copy(d, i).start()

        for i in range(2):
            mate_copy(d, i).wait_recv()
            if d:
                cross_send[d, i] = (own_sum[d, i] + mate_recv[d, i].astype(F32)).astype(BF16)
                cross_copy(d, i).start()
            else:
                own_sum[0, i] = own_sum[0, i] + mate_recv[0, i].astype(F32)
    for d in range(1, chips):
        for i in range(2):
            cross_copy(d, i).wait_recv()
    total = own_sum[0]
    for d in range(1, chips):
        total = total + cross_recv[d].astype(F32)
    gate, up = total[0], total[1]
    hid[pl.ds(r, 1)] = ((gate / (1.0 + jnp.exp(-gate))) * up).astype(BF16)[None]

    def hid_copy(d, src, at, target, ssem, rsem):
        return pltpu.make_async_remote_copy(
            src_ref=hid.at[src],
            dst_ref=hid.at[at],
            send_sem=ssem.at[d],
            recv_sem=rsem.at[d],
            device_id={"dp": target},
            device_id_type=MESH,
        )

    hid_out, hid_in = [], []
    for d in range(1, chips):
        ahead = lax.rem(chip + d, chips) * 2 + core
        behind = lax.rem(chip + chips - d, chips) * 2 + core
        hid_out.append(hid_copy(d, r, r, ahead, hid_ssem, hid_rsem))
        hid_in.append(hid_copy(d, r, behind, ahead, hid_ssem, hid_rsem))
    for copy in hid_out:
        copy.start()
    mate_r = chip * 2 + 1 - core
    mate_out = hid_copy(0, r, r, mate_r, fwd_ssem, fwd_rsem)
    mate_in = hid_copy(0, r, mate_r, mate_r, fwd_ssem, fwd_rsem)
    mate_out.start()

    ret_copies = exchange(ret_send, ret_recv, ret_ssem, ret_rsem)

    def give_back(pr):
        out = dot(hid[pr], down_t[...])
        for pe in range(experts):
            ret_send[pr * experts + pe] = slab(out[pe * CAP : (pe + 1) * CAP])

    def send_back(dr_pr, skip_self):
        for de in range(experts):
            if skip_self and de == 0:
                continue
            pe = lax.rem(e + de, experts)
            n = dr_pr * experts + pe
            pltpu.make_async_remote_copy(
                src_ref=ret_send.at[n],
                dst_ref=ret_recv.at[me],
                send_sem=ret_ssem.at[n],
                recv_sem=ret_rsem.at[me],
                device_id={"expert": pe, "dp": dr_pr},
                device_id_type=MESH,
            ).start()

    give_back(r)
    send_back(r, True)
    ret_recv[pl.ds(me, 1)] = ret_send[pl.ds(me, 1)]
    mate_in.wait_recv()
    give_back(mate_r)
    send_back(mate_r, False)
    forwards = []
    for d in range(1, chips):
        hid_in[d - 1].wait_recv()
        behind = lax.rem(chip + chips - d, chips)
        out = hid_copy(d, behind * 2 + core, behind * 2 + core, mate_r, fwd_ssem, fwd_rsem)
        into = hid_copy(d, behind * 2 + core, behind * 2 + 1 - core, mate_r, fwd_ssem, fwd_rsem)
        out.start()
        forwards.append((out, into))
        give_back(behind * 2 + core)
        send_back(behind * 2 + core, False)
    for d in range(1, chips):
        forwards[d - 1][1].wait_recv()
        behind = lax.rem(chip + chips - d, chips)
        give_back(behind * 2 + 1 - core)
        send_back(behind * 2 + 1 - core, False)

    for _, back in grad_copies:
        back.wait_recv()
    hidden = hid[...].reshape(replicas * rows, ff)
    for h in range(2):
        g = grad_recv[:, h * CAP : (h + 1) * CAP].reshape(replicas * rows, half)
        down_grad[h * half : (h + 1) * half] = dot(g, hidden, ((0,), (0,))).astype(BF16)

    arrivals = [r, mate_r]
    for d in range(1, chips):
        arrivals.append(lax.rem(chip + chips - d, chips) * 2 + core)
    for d in range(1, chips):
        arrivals.append(lax.rem(chip + chips - d, chips) * 2 + 1 - core)
    for number, pr in enumerate(arrivals):
        for de in range(1 if number == 0 else 0, experts):
            n = pr * experts + lax.rem(e + de, experts)
            pltpu.make_async_remote_copy(
                src_ref=ret_send.at[n],
                dst_ref=ret_recv.at[n],
                send_sem=ret_ssem.at[n],
                recv_sem=ret_rsem.at[n],
                device_id={"expert": lax.rem(e + de, experts), "dp": pr},
                device_id_type=MESH,
            ).wait_recv()
        arrived = ret_recv[pl.ds(pr * experts, experts)]
        for h in range(2):
            block = arrived[:, h * CAP : (h + 1) * CAP]
            block = block.reshape(rows, half)
            value = weights[0] * dot(picks[0], block, ((0,), (0,)))
            for k in range(1, top):
                value = value + weights[k] * dot(picks[k], block, ((0,), (0,)))
            start = pl.multiple_of(pr * width + h * half, 128)
            mixed[:, pl.ds(start, half)] = value.astype(BF16)

    for copies in (tok_copies, grad_copies, ret_copies):
        for out, _ in copies:
            out.wait_send()
    for i in range(2):
        for d in range(chips):
            mate_copy(d, i).wait_send()
        for d in range(1, chips):
            cross_copy(d, i).wait_send()
    for copy in hid_out:
        copy.wait_send()
    mate_out.wait_send()
    for out, _ in forwards:
        out.wait_send()


def tokens_move(tokens, out_grad, expert_ids, combine, gate_weight, up_weight, down_t):
    experts, replicas = lax.axis_size("expert"), lax.axis_size("dp")
    _, width, ff = gate_weight.shape
    top = expert_ids.shape[1]
    peers, chips, rows = experts * replicas, replicas // 2, experts * CAP
    slabs = pltpu.VMEM((peers, 2 * CAP, width // 2), BF16)
    dma = pltpu.SemaphoreType.DMA
    hbm = pl.BlockSpec(memory_space=pl.ANY)
    mixed, down_grad = pl.pallas_call(
        functools.partial(kernel, experts, replicas),
        out_shape=(
            pltpu.VMEM(tokens.shape, BF16),
            pltpu.VMEM((width, ff), BF16),
        ),
        in_specs=[hbm] * 7,
        out_specs=(pl.BlockSpec(memory_space=pltpu.VMEM),) * 2,
        scratch_shapes=[pltpu.VMEM((width, ff), BF16)] * 3
        + [pltpu.VMEM(tokens.shape, BF16)] * 2
        + [pltpu.VMEM((top, tokens.shape[0]), jnp.int32)]
        + [pltpu.VMEM((top, tokens.shape[0]), F32)]
        + [pltpu.VMEM((ff, width), BF16)]
        + [slabs] * 6
        + [pltpu.VMEM((chips, 2, rows, ff), BF16)] * 4
        + [pltpu.VMEM((chips, 2, rows, ff), F32), pltpu.VMEM((replicas, rows, ff), BF16)]
        + [dma((7,))]
        + [dma((peers,))] * 6
        + [dma((chips, 2))] * 4
        + [dma((chips,))] * 4,
        compiler_params=pltpu.CompilerParams(
            collective_id=0, has_side_effects=True, vmem_limit_bytes=60 * 1024 * 1024
        ),
    )(tokens, out_grad, expert_ids.T, combine.T, gate_weight[0], up_weight[0], down_t[0])
    return mixed, down_grad[None]


def weights_move(tokens, out_grad, expert_ids, combine, gate_weight, up_weight, down_t):
    experts = lax.axis_size("expert")
    tok_count, top_count = expert_ids.shape
    model_width = tokens.shape[1]
    slot_total = experts * CAP
    flat_ids = expert_ids.reshape(-1)
    onehot = (flat_ids[:, None] == jnp.arange(experts, dtype=jnp.int32)[None, :]).astype(jnp.int32)
    earlier = jnp.sum((jnp.cumsum(onehot, 0) - onehot) * onehot, 1)
    target = flat_ids * CAP + earlier
    sources = jnp.arange(tok_count * top_count, dtype=jnp.int32) // top_count
    slot_token = jnp.full((slot_total,), tok_count, jnp.int32).at[target].set(sources)
    slot_weight = jnp.zeros((slot_total,), jnp.float32).at[target].set(combine.reshape(-1))
    padded_rows = jnp.concatenate([tokens, jnp.zeros((1, model_width), jnp.bfloat16)], 0)
    padded_grad = jnp.concatenate([out_grad, jnp.zeros((1, model_width), jnp.bfloat16)], 0)
    send_rows = padded_rows[slot_token].reshape(experts, CAP, model_width)
    send_grad = (slot_weight[:, None] * padded_grad[slot_token].astype(jnp.float32)).astype(
        jnp.bfloat16
    )
    send_grad = send_grad.reshape(experts, CAP, model_width)
    recv_rows = lax.all_to_all(send_rows, "expert", split_axis=0, concat_axis=0, tiled=True)
    expert_rows = recv_rows.reshape(slot_total, model_width)
    gate_shard = gate_weight[0]
    up_shard = up_weight[0]
    down_shard = down_t[0]

    def add_rows(shard_piece):
        return jnp.dot(expert_rows, shard_piece, preferred_element_type=jnp.float32)

    gate_sum = add_rows(lax.all_gather(gate_shard, "dp", axis=0, tiled=True))
    up_sum = add_rows(lax.all_gather(up_shard, "dp", axis=0, tiled=True))
    hidden = (jax.nn.silu(gate_sum) * up_sum).astype(jnp.bfloat16)
    product = lax.dot_general(
        hidden,
        lax.all_gather(down_shard, "dp", axis=0, tiled=True),
        (((1,), (1,)), ((), ())),
        preferred_element_type=jnp.float32,
    )
    expert_out = product.astype(jnp.bfloat16)
    returned = lax.all_to_all(
        expert_out.reshape(experts, CAP, model_width),
        "expert",
        split_axis=0,
        concat_axis=0,
        tiled=True,
    )
    returned = returned.reshape(slot_total, model_width)[target]
    mixed = jnp.sum(
        returned.reshape(tok_count, top_count, model_width).astype(jnp.float32)
        * combine[:, :, None],
        1,
    )
    mixed = mixed.astype(jnp.bfloat16)
    recv_grad = lax.all_to_all(send_grad, "expert", split_axis=0, concat_axis=0, tiled=True)
    grad_rows = recv_grad.reshape(slot_total, model_width)
    own_grad = lax.psum_scatter(
        lax.dot_general(
            grad_rows, hidden, (((0,), (0,)), ((), ())), preferred_element_type=jnp.float32
        ).astype(jnp.bfloat16),
        "dp",
        scatter_dimension=0,
        tiled=True,
    )
    down_grad = own_grad[None]
    return (mixed, down_grad)


def solution(mesh):
    in_specs = (
        P(("group", "expert", "dp"), None),
        P(("group", "expert", "dp"), None),
        P(("group", "expert", "dp"), None),
        P(("group", "expert", "dp"), None),
        P("expert", "dp", None),
        P("expert", "dp", None),
        P("expert", "dp", None),
    )
    out_specs = (P(("group", "expert", "dp"), None), P(("group", "expert"), "dp", None))

    def per_device(*args):
        experts, replicas = lax.axis_size("expert"), lax.axis_size("dp")
        features, ff = args[0].shape[1], args[4].shape[2]
        slots = experts * replicas * CAP
        moved_tokens = slots * (3 * features // replicas + 3 * ff)
        moved_weights = 4 * features * ff + 3 * experts * CAP * features
        small = moved_tokens < moved_weights and slots <= 1024
        if small and replicas % 2 == 0 and features % (256 * replicas) == 0:
            return tokens_move(*args)
        return weights_move(*args)

    return jax.shard_map(
        per_device, mesh=mesh, in_specs=in_specs, out_specs=out_specs, check_vma=False
    )
```
